32 devices in a mesh: grp: 2 (over x), freq: 16 (over z, y, core).
Axes of the slice: x: 2, y: 2, z: 4, core: 2. Of those that a mesh axis runs over, the one named last changes fastest.
Arguments:
- start_field: bfloat16 [512, 384, 512], P(('grp', 'freq')), parts along dimension 0, may hold values from -2.390625 to 2.390625
- recorded: bfloat16 [32, 384, 4, 128], P(('grp', 'freq')), parts along dimension 0, may hold values from -6 to 6
- multiples: bfloat16 [32, 4, 3, 64, 128], P(('grp', 'freq')), parts along dimension 0, may hold values from -0.3125 to 0.3125
- block_index: int32 [4, 3], replicated, may hold values from 0 to 3, all different within a row
- radius: int32 [512, 384], P(('grp', 'freq')), parts along dimension 0, may hold values from 0 to 4
Outputs:
- field: float32 [512, 384, 512], P(('grp', 'freq')), parts along dimension 0
- residual: float32 [32, 384, 4, 128], P(('grp', 'freq')), parts along dimension 0
The draws below stay inside these ranges and needn't reach their ends.
There are 2 independent parts, one for each index of `grp`. The reference program is written for one: setup_inputs(seed, part) draws one part's arguments, and reference() takes and returns one part's arrays. A program takes and returns all parts, laid end to end along the dimension named above; an argument that names none is the same for every part. Nothing has to cross between parts.
Inputs may be any that keep to these rules, and one draw needn't show every extreme that they name: `block_index`: each row names 3 different source blocks, and every block is named by some row.
All inputs are finite; a program needn't handle non-finite values.
Results may differ from the reference program's by a relative error of at most 0.004.
Values may be sent and summed in bfloat16 or wider, within the bound.
No kernel may reach another device: no remote copies, remote signals or barrier semaphores. Data moves between devices by JAX's collectives and lax.ppermute only.
A program may use at most 64 MiB of HBM per device.

```python
import math
import jax
import jax.numpy as jnp
from jax import lax

NB = 4
BS = 64
BANDS = 3
NT = 512
RADIUS = 4
ITERS = 2
RECV = 384
S = 256
FREQ = 16


def draw_radius(key, part):
    uniform_pick = jax.random.randint(key, (S, RECV), 0, RADIUS + 1)
    source_ids = jnp.arange(S, dtype=jnp.int32)[:, None]
    receiver_ids = jnp.arange(RECV, dtype=jnp.int32)[None, :]
    return jnp.where((source_ids * 7 + receiver_ids) % 11 == 0, RADIUS, uniform_pick).astype(jnp.int32)


def shard_levels(key, shape, shards, least, top_value):
    factor_of, own = 1.0, jax.random.fold_in(key, 6)
    for dim, blocks in shards:
        steps = jnp.exp(jax.random.uniform(jax.random.fold_in(own, dim), (blocks,), jnp.float32, least / len(shards), top_value / len(shards)))
        factor_of = factor_of * jnp.repeat(steps, shape[dim] // blocks).reshape([-1 if axis == dim else 1 for axis in range(len(shape))])
    return factor_of


def picks_of(own_key, rows, amount, top, lift):
    order = jax.random.permutation(jax.random.fold_in(own_key, 1), amount)
    boost = order
    for power in range(3):
        boost = boost * boost // amount
    boost = boost * lift // amount
    tickets = jax.random.randint(jax.random.fold_in(own_key, 2), (rows, amount), 0, 4096) + boost
    fixed_rows = jax.random.permutation(jax.random.fold_in(own_key, 3), rows)[jnp.arange(amount) % rows]
    tickets = jnp.where(jnp.arange(rows)[:, None] == fixed_rows[None, :], 1 << 14, tickets)
    merit = tickets * amount + jnp.arange(amount)
    return lax.top_k(merit.astype(jnp.int32), top)[1].astype(jnp.int32)


def bell_draw(key, extent, spread, most, cuts=(), kind=jnp.bfloat16):
    array = jax.random.normal(key, extent, jnp.float32) * spread
    if len(cuts) > 0:
        array = shard_levels(key, extent, cuts, -0.22, 0.18) * array
    return jnp.clip(array, min=-most, max=most).astype(kind)


def setup_inputs(seed: int = 0, part: int = 0) -> dict:
    arg_keys = jax.random.split(jax.random.key(seed), 6)
    own_keys = jax.random.split(jax.random.fold_in(arg_keys[5], part), 6)
    start_field = bell_draw(own_keys[0], (S, RECV, NT), 0.3, 2.390625, ((0, 16),))
    recorded = bell_draw(own_keys[1], (FREQ, RECV, NB, 2 * BS), 1.0, 6.0, ((0, 16),))
    multiples = bell_draw(own_keys[2], (FREQ, NB, BANDS, BS, 2 * BS), (2 * BANDS * BS) ** -0.5, 0.3125, ((0, 16),))
    block_index = picks_of(arg_keys[3], NB, NB, BANDS, 0)
    radius = draw_radius(jax.random.fold_in(jax.random.fold_in(arg_keys[5], part), 71), part)
    return dict(start_field=start_field, recorded=recorded, multiples=multiples, block_index=block_index, radius=radius)


step_size = 0.5
shrinkage = 0.05

def dft_table(freq_count):
    sample_ids = jnp.arange(NT, dtype=jnp.int32)
    bin_ids = jnp.arange(freq_count, dtype=jnp.int32) + 1
    phases = sample_ids[:, None] * bin_ids[None, :] % NT
    angles = phases.astype(jnp.float32) * (2.0 * math.pi / NT)
    stacked = jnp.stack([jnp.cos(angles), -jnp.sin(angles)], axis=-1)
    return stacked.reshape(NT, 2 * freq_count) / math.sqrt(NT)

def embed_complex(multiples):
    real_part = multiples[..., :BS]
    imag_part = multiples[..., BS:]
    upper_rows = jnp.concatenate([real_part, imag_part], axis=-1)
    lower_rows = jnp.concatenate([-imag_part, real_part], axis=-1)
    return jnp.concatenate([upper_rows, lower_rows], axis=-2)

def owner_layout(arrived, freq_count):
    shaped = arrived.reshape(freq_count, 2, NB, BS, arrived.shape[2])
    return shaped.transpose(0, 4, 2, 1, 3).reshape(freq_count, arrived.shape[2], NB, 2 * BS)

def trace_layout(backward, freq_count):
    shaped = backward.reshape(freq_count, backward.shape[1], NB, 2, BS)
    return shaped.transpose(0, 3, 2, 4, 1).reshape(2 * freq_count, NB * BS, backward.shape[1])

def smooth_along(extended, radius, rows_out, along):
    shares = 1.0 / (2.0 * radius.astype(jnp.float32) + 1.0)
    summed = None
    for offset in range(-RADIUS, RADIUS + 1):
        weight = jnp.where(abs(offset) <= radius, shares, 0.0)
        if along == 0:
            weight = weight[:, :, None]
        else:
            weight = weight[None, :, :]
        piece = lax.slice_in_dim(extended, RADIUS + offset, RADIUS + offset + rows_out, axis=along)
        term = weight * piece.astype(jnp.float32)
        summed = term if summed is None else summed + term
    return summed

def reference(start_field, recorded, multiples, block_index, radius):
    basis = dft_table(FREQ)
    operator = embed_complex(multiples).astype(jnp.float32)
    field = start_field.astype(jnp.float32)
    residual = None
    for sweep in range(ITERS):
        spectra = jnp.einsum('srt,tc->csr', field, basis, precision=lax.Precision.HIGHEST).astype(jnp.bfloat16)
        spectra = lax.optimization_barrier(spectra)
        owned = owner_layout(spectra, FREQ).astype(jnp.float32)
        predicted = []
        for out_block in range(NB):
            summed = jnp.zeros((FREQ, RECV, 2 * BS), jnp.float32)
            for band_id in range(BANDS):
                source = owned[:, :, block_index[out_block, band_id]]
                summed = summed + jnp.einsum('frc,fcd->frd', source, operator[:, out_block, band_id])
            predicted.append(summed)
        residual = recorded.astype(jnp.float32) - jnp.stack(predicted, axis=2)
        narrow = lax.optimization_barrier(residual.astype(jnp.bfloat16)).astype(jnp.float32)
        backward = jnp.zeros((FREQ, RECV, NB, 2 * BS), jnp.float32)
        for out_block in range(NB):
            for band_id in range(BANDS):
                contrib = jnp.einsum('frd,fcd->frc', narrow[:, :, out_block], operator[:, out_block, band_id])
                backward = backward.at[:, :, block_index[out_block, band_id]].add(contrib)
        returned = lax.optimization_barrier(trace_layout(backward.astype(jnp.bfloat16), FREQ)).astype(jnp.float32)
        gradient = jnp.einsum('csr,tc->srt', returned, basis, precision=lax.Precision.HIGHEST)
        extended = jnp.pad(gradient, ((RADIUS, RADIUS), (0, 0), (0, 0)))
        smoothed = smooth_along(extended, radius, S, 0)
        update = field + step_size * smoothed
        field = jnp.sign(update) * jnp.maximum(jnp.abs(update) - shrinkage, 0.0)
    return (field, residual)
```

```python
import math

import jax
import jax.numpy as jnp
import numpy as np
from jax import lax
from jax.experimental import pallas as pl
from jax.experimental.pallas import tpu as pltpu
from jax.sharding import PartitionSpec as P

NB = 4
BS = 64
BANDS = 3
NT = 512
RADIUS = 4
ITERS = 2
STEP = 0.5
SHRINKAGE = 0.05
MIB = 1 << 20


def split_table(freq_count):
    phases = np.arange(NT)[:, None] * (np.arange(freq_count) + 1)[None, :] % NT
    angles = phases * (2.0 * math.pi / NT)
    table = np.stack([np.cos(angles), -np.sin(angles)], axis=-1).reshape(NT, 2 * freq_count) / math.sqrt(NT)
    table = table.T.astype(np.float32)
    upper = table.astype(jnp.bfloat16)
    lower = (table - upper.astype(np.float32)).astype(jnp.bfloat16)
    return np.concatenate([upper, lower], axis=0)


def contract(a, b, dims):
    return lax.dot_general(a, b, ((dims[:1], dims[1:]), ((), ())), preferred_element_type=jnp.float32)


def shrink(u):
    return u - jnp.clip(u, -SHRINKAGE, SHRINKAGE)


def params(semantics, limit):
    return pltpu.CompilerParams(dimension_semantics=(semantics,), vmem_limit_bytes=limit * MIB)


def rows_per_step(rows, receivers):
    step = receivers
    while step * 2 <= 1024 and rows % (step * 2) == 0:
        step *= 2
    return step


def forward_kernel(field_ref, table_ref, spectra_ref):
    half = spectra_ref.shape[0]
    both = contract(table_ref[...], field_ref[...], (1, 1))
    spectra_ref[...] = (both[:half] + both[half:]).astype(jnp.bfloat16)


def forward(field, table, receivers):
    rows = field.shape[0]
    step = rows_per_step(rows, receivers)
    count = table.shape[0] // 2
    return pl.pallas_call(
        forward_kernel,
        grid=(rows // step,),
        in_specs=[pl.BlockSpec((step, NT), lambda i: (i, 0)), pl.BlockSpec(table.shape, lambda i: (0, 0))],
        out_specs=pl.BlockSpec((count, step), lambda i: (0, i)),
        out_shape=jax.ShapeDtypeStruct((count, rows), jnp.bfloat16),
        compiler_params=params("arbitrary", 16),
        cost_estimate=pl.CostEstimate(flops=4 * rows * NT * count, bytes_accessed=2 * rows * NT, transcendentals=0),
        name="forward_dft",
    )(field, table)


def gradient_of(spectra_ref, half_table_ref):
    spectra = spectra_ref[...]
    return contract(jnp.concatenate([spectra, spectra], axis=0), half_table_ref[...], (0, 0))


def middle_kernel(start_ref, spectra_ref, table_ref, half_table_ref, field_ref, out_ref):
    count = out_ref.shape[0]
    field = shrink(start_ref[...].astype(jnp.float32) + gradient_of(spectra_ref, half_table_ref))
    field_ref[...] = field
    upper = field.astype(jnp.bfloat16)
    lower = (field - upper.astype(jnp.float32)).astype(jnp.bfloat16)
    both = contract(table_ref[...], upper, (1, 1))
    rest = contract(table_ref[:count], lower, (1, 1))
    out_ref[...] = (both[:count] + (both[count:] + rest)).astype(jnp.bfloat16)


def middle(start, spectra, table, half_table, receivers):
    rows = start.shape[0]
    step = rows_per_step(rows, receivers)
    count = table.shape[0] // 2
    return pl.pallas_call(
        middle_kernel,
        grid=(rows // step,),
        in_specs=[
            pl.BlockSpec((step, NT), lambda i: (i, 0)),
            pl.BlockSpec((count, step), lambda i: (0, i)),
            pl.BlockSpec(table.shape, lambda i: (0, 0)),
            pl.BlockSpec(half_table.shape, lambda i: (0, 0)),
        ],
        out_specs=[pl.BlockSpec((step, NT), lambda i: (i, 0)), pl.BlockSpec((count, step), lambda i: (0, i))],
        out_shape=[jax.ShapeDtypeStruct((rows, NT), jnp.float32), jax.ShapeDtypeStruct((count, rows), jnp.bfloat16)],
        compiler_params=params("arbitrary", 24),
        cost_estimate=pl.CostEstimate(flops=10 * rows * NT * count, bytes_accessed=6 * rows * NT, transcendentals=0),
        name="update_and_forward",
    )(start, spectra, table, half_table)


def final_kernel(field_ref, spectra_ref, half_table_ref, out_ref):
    out_ref[...] = shrink(field_ref[...] + gradient_of(spectra_ref, half_table_ref))


def final(field, spectra, half_table, receivers):
    rows = field.shape[0]
    step = rows_per_step(rows, receivers)
    count = half_table.shape[0] // 2
    return pl.pallas_call(
        final_kernel,
        grid=(rows // step,),
        in_specs=[
            pl.BlockSpec((step, NT), lambda i: (i, 0)),
            pl.BlockSpec((count, step), lambda i: (0, i)),
            pl.BlockSpec(half_table.shape, lambda i: (0, 0)),
        ],
        out_specs=pl.BlockSpec((step, NT), lambda i: (i, 0)),
        out_shape=jax.ShapeDtypeStruct((rows, NT), jnp.float32),
        compiler_params=params("arbitrary", 24),
        cost_estimate=pl.CostEstimate(flops=4 * rows * NT * count, bytes_accessed=8 * rows * NT, transcendentals=0),
        name="last_update",
    )(field, spectra, half_table)


def owner_kernel(index_ref, arrived_ref, recorded_ref, multiples_ref, radius_ref, *rest):
    returned_ref, operator, padded = rest[0], rest[-2], rest[-1]
    sources = NB * BS
    operator[...] = jnp.zeros_like(operator)
    for block in range(NB):
        columns = slice(block * 2 * BS, (block + 1) * 2 * BS)
        for band in range(BANDS):
            first = pl.multiple_of(index_ref[block, band] * BS, BS)
            pair = multiples_ref[0, block, band]
            operator[pl.ds(first, BS), columns] = pair
            operator[pl.ds(sources + first, BS), columns] = jnp.concatenate([-pair[:, BS:], pair[:, :BS]], axis=1)
    table = operator[...]
    residual = recorded_ref[0].astype(jnp.float32) - contract(arrived_ref[0], table, (0, 0))
    if len(rest) == 4:
        rest[1][0] = residual
    backward = contract(table, residual.astype(jnp.bfloat16), (1, 1))
    radius = radius_ref[...]
    shares = 1.0 / (2.0 * radius.astype(jnp.float32) + 1.0)
    for part in range(2):
        own = backward[part * sources : (part + 1) * sources]
        padded[: 2 * RADIUS] = jnp.zeros_like(padded[: 2 * RADIUS])
        padded[2 * RADIUS + sources :] = jnp.zeros_like(padded[: 2 * RADIUS])
        padded[2 * RADIUS : 2 * RADIUS + sources] = own
        summed = own
        for offset in range(1, RADIUS + 1):
            low = padded[2 * RADIUS - offset : 2 * RADIUS - offset + sources]
            high = padded[2 * RADIUS + offset : 2 * RADIUS + offset + sources]
            summed = summed + jnp.where(radius >= offset, low + high, 0.0)
        returned_ref[0, part] = (summed * shares).astype(jnp.bfloat16)


def owner(arrived, recorded, multiples, block_index, radius, with_residual):
    count, _, receivers = arrived.shape
    sources = NB * BS
    wide = NB * 2 * BS
    out_specs = [pl.BlockSpec((1, 2, sources, receivers), lambda i: (i, 0, 0, 0))]
    out_shape = [jax.ShapeDtypeStruct((count, 2, sources, receivers), jnp.bfloat16)]
    if with_residual:
        out_specs.append(pl.BlockSpec((1, receivers, wide), lambda i: (i, 0, 0)))
        out_shape.append(jax.ShapeDtypeStruct((count, receivers, wide), jnp.float32))
    return pl.pallas_call(
        owner_kernel,
        grid=(count,),
        in_specs=[
            pl.BlockSpec(memory_space=pltpu.SMEM),
            pl.BlockSpec((1, 2 * sources, receivers), lambda i: (i, 0, 0)),
            pl.BlockSpec((1, receivers, wide), lambda i: (i, 0, 0)),
            pl.BlockSpec((1, NB, BANDS, BS, 2 * BS), lambda i: (i, 0, 0, 0, 0)),
            pl.BlockSpec((sources, receivers), lambda i: (0, 0)),
        ],
        out_specs=out_specs,
        out_shape=out_shape,
        scratch_shapes=[
            pltpu.VMEM((2 * sources, wide), jnp.bfloat16),
            pltpu.VMEM((sources + 4 * RADIUS, receivers), jnp.float32),
        ],
        compiler_params=params("arbitrary", 24),
        cost_estimate=pl.CostEstimate(
            flops=8 * count * receivers * sources * wide, bytes_accessed=6 * count * receivers * wide, transcendentals=0
        ),
        name="owner_step",
    )(block_index, arrived, recorded, multiples, radius)


def on_device(start_field, recorded, multiples, block_index, radius):
    devices = lax.axis_size("freq")
    local_freq = recorded.shape[0]
    all_freq = local_freq * devices
    local_src, receivers, _ = start_field.shape
    rows = local_src * receivers
    table = jnp.asarray(split_table(all_freq))
    half_table = table * STEP
    start = start_field.reshape(rows, NT)
    recorded = recorded.reshape(local_freq, receivers, NB * 2 * BS)
    radius = lax.all_gather(radius, "freq", axis=0, tiled=True)
    field, residual = start, None
    spectra = forward(start, table, receivers)
    for sweep in range(ITERS):
        last = sweep == ITERS - 1
        arrived = lax.all_to_all(
            spectra.reshape(2 * all_freq, local_src, receivers), "freq", split_axis=0, concat_axis=1, tiled=True
        )
        outs = owner(
            arrived.reshape(local_freq, 2 * NB * BS, receivers), recorded, multiples, block_index, radius, last
        )
        returned = lax.all_to_all(
            outs[0].reshape(2 * local_freq, NB * BS, receivers), "freq", split_axis=1, concat_axis=0, tiled=True
        ).reshape(2 * all_freq, rows)
        if last:
            field = final(field, returned, half_table, receivers)
            residual = outs[1]
        else:
            field, spectra = middle(field, returned, table, half_table, receivers)
    return (
        field.reshape(local_src, receivers, NT),
        residual.reshape(local_freq, receivers, NB, 2 * BS),
    )


def solution(mesh):
    placed = (
        P(("grp", "freq"), None, None),
        P(("grp", "freq"), None, None, None),
        P(("grp", "freq"), None, None, None, None),
        P(),
        P(("grp", "freq"), None),
    )
    return jax.shard_map(
        on_device,
        mesh=mesh,
        in_specs=placed,
        out_specs=(P(("grp", "freq"), None, None), P(("grp", "freq"), None, None, None)),
        check_vma=False,
    )
```

```python
import math

import jax
import jax.numpy as jnp
import numpy as np
from jax import lax
from jax.experimental import pallas as pl
from jax.experimental.pallas import tpu as pltpu
from jax.sharding import PartitionSpec as P

NB = 4
BS = 64
BANDS = 3
NT = 512
RADIUS = 4
STEP = 0.5
SHRINKAGE = 0.05
SOURCES = NB * BS
WIDE = NB * 2 * BS
MIB = 1 << 20
VMEM = pl.BlockSpec(memory_space=pltpu.VMEM)
ANY = pl.BlockSpec(memory_space=pl.ANY)


def split_table(freq_count):
    phases = np.arange(NT)[:, None] * (np.arange(freq_count) + 1)[None, :] % NT
    angles = phases * (2.0 * math.pi / NT)
    table = np.stack([np.cos(angles), -np.sin(angles)], axis=-1).reshape(NT, 2 * freq_count) / math.sqrt(NT)
    table = table.T.astype(np.float32)
    upper = table.astype(jnp.bfloat16)
    lower = (table - upper.astype(np.float32)).astype(jnp.bfloat16)
    return np.concatenate([upper, lower], axis=0)


def contract(a, b, dims):
    return lax.dot_general(a, b, ((dims[:1], dims[1:]), ((), ())), preferred_element_type=jnp.float32)


def clamp(u):
    return jnp.clip(u, -SHRINKAGE, SHRINKAGE)


def params(limit):
    return pltpu.CompilerParams(vmem_limit_bytes=limit * MIB)


def chunk_rows(rows, most):
    return max(size for size in range(128, most + 1, 128) if rows % size == 0)


def build_operator(index_ref, multiples_ref, operator_ref):
    operator_ref[...] = jnp.zeros_like(operator_ref)
    for block in range(NB):
        columns = slice(block * 2 * BS, (block + 1) * 2 * BS)
        for band in range(BANDS):
            first = pl.multiple_of(index_ref[block, band] * BS, BS)
            pair = multiples_ref[block, band]
            operator_ref[pl.ds(first, BS), columns] = pair
            operator_ref[pl.ds(SOURCES + first, BS), columns] = jnp.concatenate([-pair[:, BS:], pair[:, :BS]], axis=1)


def forward_kernel(
    field_hbm, table_hbm, index_hbm, multiples_hbm, recorded_hbm, radius_hbm,
    narrow_ref, spectra_ref, field_ref, table_ref, operator_ref, recorded_ref, radius_ref,
    index, multiples, loaded, unpacked, radius, sems, field_sems,
):
    receivers = recorded_ref.shape[0]
    count, rows = spectra_ref.shape
    step = rows // field_sems.shape[0]
    small = [
        pltpu.make_async_copy(index_hbm, index, sems.at[0]),
        pltpu.make_async_copy(multiples_hbm, multiples, sems.at[1]),
        pltpu.make_async_copy(recorded_hbm, loaded, sems.at[2]),
        pltpu.make_async_copy(table_hbm, table_ref, sems.at[3]),
        pltpu.make_async_copy(radius_hbm, radius, sems.at[4]),
    ]
    for copy in small:
        copy.start()
    large = []
    for i in range(rows // step):
        part = pl.ds(i * step, step)
        large.append(pltpu.make_async_copy(field_hbm.at[part], field_ref.at[part], field_sems.at[i]))
        large[-1].start()
    small[0].wait()
    small[1].wait()
    build_operator(index, multiples, operator_ref)
    small[2].wait()
    unpacked[...] = loaded[...].astype(jnp.float32)
    for block in range(NB):
        recorded_ref[:, block * 2 * BS : (block + 1) * 2 * BS] = unpacked[pl.ds(block, receivers, stride=NB), :]
    small[4].wait()
    radius_ref[...] = radius[...].astype(jnp.float32).astype(jnp.bfloat16)
    small[3].wait()
    for i in range(rows // step):
        part = slice(i * step, (i + 1) * step)
        large[i].wait()
        both = contract(table_ref[...], field_ref[part], (1, 1))
        spectra = both[:count] + both[count:]
        spectra_ref[:, part] = spectra
        narrow_ref[:, part] = spectra.astype(jnp.bfloat16)


def forward(field, table, block_index, multiples, recorded, radius):
    rows, receivers = field.shape[0], radius.shape[1]
    step = chunk_rows(rows, 1024)
    count = table.shape[0] // 2
    arguments = (field, table, block_index, multiples, recorded, radius)
    return pl.pallas_call(
        forward_kernel,
        in_specs=[ANY] * 6,
        out_specs=[VMEM] * 7,
        out_shape=[
            jax.ShapeDtypeStruct((count, rows), jnp.bfloat16),
            pltpu.VMEM((count, rows), jnp.float32),
            pltpu.VMEM((rows, NT), jnp.bfloat16),
            pltpu.VMEM(table.shape, jnp.bfloat16),
            pltpu.VMEM((2 * SOURCES, WIDE), jnp.bfloat16),
            pltpu.VMEM((receivers, WIDE), jnp.float32),
            jax.ShapeDtypeStruct(radius.shape, jnp.bfloat16),
        ],
        scratch_shapes=[
            pltpu.SMEM((NB, BANDS), jnp.int32),
            pltpu.VMEM((NB, BANDS, BS, 2 * BS), jnp.bfloat16),
            pltpu.VMEM((receivers * NB, 2 * BS), jnp.bfloat16),
            pltpu.VMEM((receivers * NB, 2 * BS), jnp.float32),
            pltpu.VMEM(radius.shape, jnp.int32),
            pltpu.SemaphoreType.DMA((5,)),
            pltpu.SemaphoreType.DMA((rows // step,)),
        ],
        compiler_params=params(16),
        name="forward_dft",
    )(*(pltpu.with_memory_space_constraint(a, pltpu.HBM) for a in arguments))


def gradient_of(returned_ref, table_ref, part):
    returned = returned_ref[:, part]
    return contract(jnp.concatenate([returned, returned], axis=0), table_ref[...], (0, 0))


def middle_kernel(start_ref, returned_ref, spectra_ref, table_ref, field_ref, narrow_ref, *, step):
    count, rows = spectra_ref.shape
    for i in range(rows // step):
        part = slice(i * step, (i + 1) * step)
        update = start_ref[part].astype(jnp.float32) + gradient_of(returned_ref, table_ref, part)
        clamped = clamp(update)
        field_ref[part] = update - clamped
        both = contract(table_ref[...], clamped.astype(jnp.bfloat16), (1, 1))
        linear = spectra_ref[:, part] + 0.5 * returned_ref[:, part].astype(jnp.float32)
        narrow_ref[:, part] = (linear - (both[:count] + both[count:])).astype(jnp.bfloat16)


def middle(start, returned, spectra, table):
    rows = start.shape[0]
    step = chunk_rows(rows, 768)
    return pl.pallas_call(
        lambda *refs: middle_kernel(*refs, step=step),
        in_specs=[VMEM] * 4,
        out_specs=[VMEM] * 2,
        out_shape=[pltpu.VMEM((rows, NT), jnp.float32), jax.ShapeDtypeStruct(spectra.shape, jnp.bfloat16)],
        compiler_params=params(16),
        name="update_and_forward",
    )(start, returned, spectra, table)


def final_kernel(field_ref, returned_ref, table_ref, out_hbm, buffer, sems):
    slots, step, _ = buffer.shape
    rows = field_ref.shape[0]
    copies = []
    for i in range(rows // step):
        if i >= slots:
            copies[i - slots].wait()
        part = slice(i * step, (i + 1) * step)
        update = field_ref[part] + gradient_of(returned_ref, table_ref, part)
        buffer[i % slots] = update - clamp(update)
        copies.append(
            pltpu.make_async_copy(buffer.at[i % slots], out_hbm.at[pl.ds(i * step, step)], sems.at[i % slots])
        )
        copies[i].start()
    for copy in copies[-slots:]:
        copy.wait()


def final(field, returned, table):
    rows = field.shape[0]
    step = chunk_rows(rows, 512)
    slots = min(4, rows // step)
    return pl.pallas_call(
        final_kernel,
        in_specs=[VMEM] * 3,
        out_specs=ANY,
        out_shape=pltpu.HBM((rows, NT), jnp.float32),
        scratch_shapes=[pltpu.VMEM((slots, step, NT), jnp.float32), pltpu.SemaphoreType.DMA((slots,))],
        compiler_params=params(16),
        name="last_update",
    )(field, returned, table)


def owner_kernel(arrived_ref, operator_ref, recorded_ref, radius_ref, returned_ref, *rest):
    with_residual = len(rest) > 1
    padded = rest[1] if with_residual else rest[0]
    receivers = recorded_ref.shape[0]
    operator = operator_ref[...]
    residual = recorded_ref[...] - contract(arrived_ref[...], operator, (0, 0))
    if with_residual:
        residual_hbm, _, interleaved, sem = rest
        for block in range(NB):
            interleaved[pl.ds(block, receivers, stride=NB), :] = residual[:, block * 2 * BS : (block + 1) * 2 * BS]
        copy = pltpu.make_async_copy(interleaved, residual_hbm, sem)
        copy.start()
    backward = contract(operator, residual.astype(jnp.bfloat16), (1, 1))
    radius = radius_ref[...].astype(jnp.float32)
    shares = STEP / (2.0 * radius + 1.0)
    edge = jnp.zeros((2 * RADIUS, receivers), jnp.float32)
    for part in range(2):
        own = backward[part * SOURCES : (part + 1) * SOURCES]
        padded[part, : 2 * RADIUS] = edge
        padded[part, 2 * RADIUS + SOURCES :] = edge
        padded[part, 2 * RADIUS : 2 * RADIUS + SOURCES] = own
        summed = own
        for offset in range(1, RADIUS + 1):
            low = padded[part, 2 * RADIUS - offset : 2 * RADIUS - offset + SOURCES]
            high = padded[part, 2 * RADIUS + offset : 2 * RADIUS + offset + SOURCES]
            summed = summed + jnp.where(radius >= offset, low + high, 0.0)
        returned_ref[part * SOURCES : (part + 1) * SOURCES] = (summed * shares).astype(jnp.bfloat16)
    if with_residual:
        copy.wait()


def owner(arrived, operator, recorded, radius, with_residual):
    receivers = arrived.shape[1]
    out_shape = [jax.ShapeDtypeStruct((2 * SOURCES, receivers), jnp.bfloat16)]
    scratch = [pltpu.VMEM((2, SOURCES + 4 * RADIUS, receivers), jnp.float32)]
    if with_residual:
        out_shape.append(pltpu.HBM((receivers * NB, 2 * BS), jnp.float32))
        scratch += [pltpu.VMEM((receivers * NB, 2 * BS), jnp.float32), pltpu.SemaphoreType.DMA(())]
    return pl.pallas_call(
        owner_kernel,
        in_specs=[VMEM] * 4,
        out_specs=[VMEM, ANY][: len(out_shape)],
        out_shape=out_shape,
        scratch_shapes=scratch,
        compiler_params=params(16),
        name="owner_step",
    )(arrived, operator, recorded, radius)


def exchange(pieces):
    return lax.all_to_all(pieces, "freq", split_axis=0, concat_axis=0, tiled=True)


def on_device(start_field, recorded, multiples, block_index, radius):
    devices = lax.axis_size("freq")
    local_src, receivers, _ = start_field.shape
    rows = local_src * receivers
    table = jnp.asarray(split_table(devices))

    def to_owners(narrow, extra=None):
        pieces = narrow.reshape(devices, 2, local_src, receivers)
        if extra is not None:
            extra = jnp.broadcast_to(extra, (devices, 1, local_src, receivers))
            pieces = jnp.concatenate([pieces, extra], axis=1)
        arrived = exchange(pieces).swapaxes(0, 1)
        return arrived.reshape(arrived.shape[0] * SOURCES, receivers)

    def to_traces(returned):
        pieces = returned.reshape(2, devices, local_src, receivers).swapaxes(0, 1)
        return exchange(pieces).reshape(2 * devices, rows)

    narrow, spectra, start, table, operator, recorded, radius = forward(
        start_field.reshape(rows, NT), table, block_index, multiples[0], recorded.reshape(-1, 2 * BS), radius
    )
    arrived = to_owners(narrow, radius)
    radius = arrived[2 * SOURCES :]
    (returned,) = owner(arrived[: 2 * SOURCES], operator, recorded, radius, False)
    field, narrow = middle(start, to_traces(returned), spectra, table)
    returned, residual = owner(to_owners(narrow), operator, recorded, radius, True)
    field = final(field, to_traces(returned), table)
    return field.reshape(local_src, receivers, NT), residual.reshape(1, receivers, NB, 2 * BS)


def solution(mesh):
    placed = (
        P(("grp", "freq"), None, None),
        P(("grp", "freq"), None, None, None),
        P(("grp", "freq"), None, None, None, None),
        P(),
        P(("grp", "freq"), None),
    )
    return jax.shard_map(
        on_device,
        mesh=mesh,
        in_specs=placed,
        out_specs=(P(("grp", "freq"), None, None), P(("grp", "freq"), None, None, None)),
        check_vma=False,
    )
```

```python
import math

import jax
import jax.numpy as jnp
import numpy as np
from jax import lax
from jax.experimental import pallas as pl
from jax.experimental.pallas import tpu as pltpu
from jax.sharding import PartitionSpec as P

NB = 4
BS = 64
BANDS = 3
NT = 512
RADIUS = 4
STEP = 0.5
SHRINKAGE = 0.05
SOURCES = NB * BS
WIDE = NB * 2 * BS
MIB = 1 << 20
VMEM = pl.BlockSpec(memory_space=pltpu.VMEM)
ANY = pl.BlockSpec(memory_space=pl.ANY)


def split_table(freq_count):
    phases = np.arange(NT)[:, None] * (np.arange(freq_count) + 1)[None, :] % NT
    angles = phases * (2.0 * math.pi / NT)
    table = np.stack([np.cos(angles), -np.sin(angles)], axis=-1).reshape(NT, 2 * freq_count) / math.sqrt(NT)
    table = table.T.astype(np.float32)
    upper = table.astype(jnp.bfloat16)
    lower = (table - upper.astype(np.float32)).astype(jnp.bfloat16)
    return np.concatenate([upper, lower], axis=0)


def contract(a, b, dims):
    return lax.dot_general(a, b, ((dims[:1], dims[1:]), ((), ())), preferred_element_type=jnp.float32)


def clamp(u):
    return jnp.clip(u, -SHRINKAGE, SHRINKAGE)


def params(limit):
    return pltpu.CompilerParams(vmem_limit_bytes=limit * MIB)


def chunk_rows(rows, most):
    return max(size for size in range(128, most + 1, 128) if rows % size == 0)


def chunks(rows):
    unit = rows // 128 // 6 * 128
    bounds = [0, unit, 2 * unit, 4 * unit, rows] if unit else [0, rows]
    return [slice(low, high) for low, high in zip(bounds[:-1], bounds[1:])]


def build_operator(index_ref, multiples_ref, operator_ref):
    operator_ref[...] = jnp.zeros_like(operator_ref)
    for block in range(NB):
        columns = slice(block * 2 * BS, (block + 1) * 2 * BS)
        for band in range(BANDS):
            first = pl.multiple_of(index_ref[block, band] * BS, BS)
            pair = multiples_ref[block, band]
            operator_ref[pl.ds(first, BS), columns] = pair
            operator_ref[pl.ds(SOURCES + first, BS), columns] = jnp.concatenate([-pair[:, BS:], pair[:, :BS]], axis=1)


def forward_kernel(
    field_hbm, table_hbm, index_hbm, multiples_hbm, recorded_hbm, radius_hbm,
    narrow_ref, spectra_ref, field_ref, table_ref, operator_ref, recorded_ref, radius_ref,
    index, multiples, loaded, unpacked, radius, sems, field_sems,
):
    receivers = recorded_ref.shape[0]
    count, rows = spectra_ref.shape
    parts = chunks(rows)
    small = [
        pltpu.make_async_copy(table_hbm, table_ref, sems.at[0]),
        pltpu.make_async_copy(index_hbm, index, sems.at[1]),
        pltpu.make_async_copy(multiples_hbm, multiples, sems.at[2]),
        pltpu.make_async_copy(recorded_hbm, loaded, sems.at[3]),
        pltpu.make_async_copy(radius_hbm, radius, sems.at[4]),
    ]
    large = []
    for i, part in enumerate(parts):
        place = pl.ds(part.start, part.stop - part.start)
        large.append(pltpu.make_async_copy(field_hbm.at[place], field_ref.at[place], field_sems.at[i]))
    for copy in small[:1] + large[:2] + small[1:] + large[2:]:
        copy.start()

    def transform(i):
        large[i].wait()
        both = contract(table_ref[...], field_ref[parts[i]], (1, 1))
        spectra = both[:count] + both[count:]
        spectra_ref[:, parts[i]] = spectra
        narrow_ref[:, parts[i]] = spectra.astype(jnp.bfloat16)

    small[0].wait()
    transform(0)
    small[1].wait()
    small[2].wait()
    build_operator(index, multiples, operator_ref)
    for i in range(1, len(parts) // 2):
        transform(i)
    small[3].wait()
    unpacked[...] = loaded[...].astype(jnp.float32)
    for block in range(NB):
        recorded_ref[:, block * 2 * BS : (block + 1) * 2 * BS] = unpacked[pl.ds(block, receivers, stride=NB), :]
    small[4].wait()
    radius_ref[...] = radius[...].astype(jnp.float32).astype(jnp.bfloat16)
    for i in range(max(1, len(parts) // 2), len(parts)):
        transform(i)


def forward(field, table, block_index, multiples, recorded, radius):
    rows, receivers = field.shape[0], radius.shape[1]
    count = table.shape[0] // 2
    arguments = (field, table, block_index, multiples, recorded, radius)
    return pl.pallas_call(
        forward_kernel,
        in_specs=[ANY] * 6,
        out_specs=[VMEM] * 7,
        out_shape=[
            jax.ShapeDtypeStruct((count, rows), jnp.bfloat16),
            pltpu.VMEM((count, rows), jnp.float32),
            pltpu.VMEM((rows, NT), jnp.bfloat16),
            pltpu.VMEM(table.shape, jnp.bfloat16),
            pltpu.VMEM((2 * SOURCES, WIDE), jnp.bfloat16),
            pltpu.VMEM((receivers, WIDE), jnp.float32),
            jax.ShapeDtypeStruct(radius.shape, jnp.bfloat16),
        ],
        scratch_shapes=[
            pltpu.SMEM((NB, BANDS), jnp.int32),
            pltpu.VMEM((NB, BANDS, BS, 2 * BS), jnp.bfloat16),
            pltpu.VMEM((receivers * NB, 2 * BS), jnp.bfloat16),
            pltpu.VMEM((receivers * NB, 2 * BS), jnp.float32),
            pltpu.VMEM(radius.shape, jnp.int32),
            pltpu.SemaphoreType.DMA((5,)),
            pltpu.SemaphoreType.DMA((len(chunks(rows)),)),
        ],
        compiler_params=params(16),
        name="forward_dft",
    )(*(pltpu.with_memory_space_constraint(a, pltpu.HBM) for a in arguments))


def gradient_of(returned_ref, table_ref, part):
    returned = returned_ref[:, part]
    return contract(jnp.concatenate([returned, returned], axis=0), table_ref[...], (0, 0))


def middle_kernel(start_ref, returned_ref, spectra_ref, table_ref, field_ref, narrow_ref, *, step):
    count, rows = spectra_ref.shape
    for i in range(rows // step):
        part = slice(i * step, (i + 1) * step)
        update = start_ref[part].astype(jnp.float32) + gradient_of(returned_ref, table_ref, part)
        clamped = clamp(update)
        field_ref[part] = update - clamped
        both = contract(table_ref[...], clamped.astype(jnp.bfloat16), (1, 1))
        linear = spectra_ref[:, part] + 0.5 * returned_ref[:, part].astype(jnp.float32)
        narrow_ref[:, part] = (linear - (both[:count] + both[count:])).astype(jnp.bfloat16)


def middle(start, returned, spectra, table):
    rows = start.shape[0]
    step = chunk_rows(rows, 768)
    return pl.pallas_call(
        lambda *refs: middle_kernel(*refs, step=step),
        in_specs=[VMEM] * 4,
        out_specs=[VMEM] * 2,
        out_shape=[pltpu.VMEM((rows, NT), jnp.float32), jax.ShapeDtypeStruct(spectra.shape, jnp.bfloat16)],
        compiler_params=params(16),
        name="update_and_forward",
    )(start, returned, spectra, table)


def final_kernel(field_ref, returned_ref, table_ref, out_hbm, buffer, sems):
    slots, step, _ = buffer.shape
    rows = field_ref.shape[0]
    copies = []
    for i in range(rows // step):
        if i >= slots:
            copies[i - slots].wait()
        part = slice(i * step, (i + 1) * step)
        update = field_ref[part] + gradient_of(returned_ref, table_ref, part)
        buffer[i % slots] = update - clamp(update)
        copies.append(
            pltpu.make_async_copy(buffer.at[i % slots], out_hbm.at[pl.ds(i * step, step)], sems.at[i % slots])
        )
        copies[i].start()
    for copy in copies[-slots:]:
        copy.wait()


def final(field, returned, table):
    rows = field.shape[0]
    step = chunk_rows(rows, 512)
    slots = min(4, rows // step)
    return pl.pallas_call(
        final_kernel,
        in_specs=[VMEM] * 3,
        out_specs=ANY,
        out_shape=pltpu.HBM((rows, NT), jnp.float32),
        scratch_shapes=[pltpu.VMEM((slots, step, NT), jnp.float32), pltpu.SemaphoreType.DMA((slots,))],
        compiler_params=params(16),
        name="last_update",
    )(field, returned, table)


def smooth(backward, radius):
    sources, receivers = radius.shape
    rows = jnp.concatenate([backward[:sources], backward[sources:]], axis=1)
    narrow = rows.astype(jnp.bfloat16)
    radius = jnp.concatenate([radius, radius], axis=1)
    distance = jnp.abs(
        lax.broadcasted_iota(jnp.int32, (sources, sources), 0) - lax.broadcasted_iota(jnp.int32, (sources, sources), 1)
    )
    summed = rows
    for width in range(1, RADIUS + 1):
        band = jnp.where(distance <= width, 1.0, 0.0).astype(jnp.bfloat16)
        summed = jnp.where(radius >= width, contract(band, narrow, (1, 0)), summed)
    smoothed = (summed * (STEP / (2.0 * radius + 1.0))).astype(jnp.bfloat16)
    return jnp.concatenate([smoothed[:, :receivers], smoothed[:, receivers:]], axis=0)


def owner_kernel(arrived_ref, operator_ref, recorded_ref, radius_ref, returned_ref, *rest):
    with_residual = len(rest) > 0
    receivers = recorded_ref.shape[0]
    operator = operator_ref[...]
    residual = recorded_ref[...] - contract(arrived_ref[...], operator, (0, 0))
    if with_residual:
        residual_hbm, interleaved, sem = rest
        for block in range(NB):
            interleaved[pl.ds(block, receivers, stride=NB), :] = residual[:, block * 2 * BS : (block + 1) * 2 * BS]
        copy = pltpu.make_async_copy(interleaved, residual_hbm, sem)
        copy.start()
    backward = contract(operator, residual.astype(jnp.bfloat16), (1, 1))
    returned_ref[...] = smooth(backward, radius_ref[...].astype(jnp.float32))
    if with_residual:
        copy.wait()


def owner(arrived, operator, recorded, radius, with_residual):
    receivers = arrived.shape[1]
    out_shape = [jax.ShapeDtypeStruct((2 * SOURCES, receivers), jnp.bfloat16)]
    scratch = []
    if with_residual:
        out_shape.append(pltpu.HBM((receivers * NB, 2 * BS), jnp.float32))
        scratch = [pltpu.VMEM((receivers * NB, 2 * BS), jnp.float32), pltpu.SemaphoreType.DMA(())]
    return pl.pallas_call(
        owner_kernel,
        in_specs=[VMEM] * 4,
        out_specs=[VMEM, ANY][: len(out_shape)],
        out_shape=out_shape,
        scratch_shapes=scratch,
        compiler_params=params(16),
        name="owner_step",
    )(arrived, operator, recorded, radius)


def exchange(pieces):
    return lax.all_to_all(pieces, "freq", split_axis=0, concat_axis=0, tiled=True)


def on_device(start_field, recorded, multiples, block_index, radius):
    devices = lax.axis_size("freq")
    local_src, receivers, _ = start_field.shape
    rows = local_src * receivers
    table = jnp.asarray(split_table(devices))

    def to_owners(narrow, extra=None):
        pieces = narrow.reshape(devices, 2, local_src, receivers)
        if extra is not None:
            extra = jnp.broadcast_to(extra, (devices, 1, local_src, receivers))
            pieces = jnp.concatenate([pieces, extra], axis=1)
        arrived = exchange(pieces).swapaxes(0, 1)
        return arrived.reshape(arrived.shape[0] * SOURCES, receivers)

    def to_traces(returned):
        pieces = returned.reshape(2, devices, local_src, receivers).swapaxes(0, 1)
        return exchange(pieces).reshape(2 * devices, rows)

    narrow, spectra, start, table, operator, recorded, radius = forward(
        start_field.reshape(rows, NT), table, block_index, multiples[0], recorded.reshape(-1, 2 * BS), radius
    )
    arrived = to_owners(narrow, radius)
    radius = arrived[2 * SOURCES :]
    (returned,) = owner(arrived[: 2 * SOURCES], operator, recorded, radius, False)
    field, narrow = middle(start, to_traces(returned), spectra, table)
    returned, residual = owner(to_owners(narrow), operator, recorded, radius, True)
    field = final(field, to_traces(returned), table)
    return field.reshape(local_src, receivers, NT), residual.reshape(1, receivers, NB, 2 * BS)


def solution(mesh):
    placed = (
        P(("grp", "freq"), None, None),
        P(("grp", "freq"), None, None, None),
        P(("grp", "freq"), None, None, None, None),
        P(),
        P(("grp", "freq"), None),
    )
    return jax.shard_map(
        on_device,
        mesh=mesh,
        in_specs=placed,
        out_specs=(P(("grp", "freq"), None, None), P(("grp", "freq"), None, None, None)),
        check_vma=False,
    )
```

```python
import math

import jax
import jax.numpy as jnp
import numpy as np
from jax import lax
from jax.experimental import pallas as pl
from jax.experimental.pallas import tpu as pltpu
from jax.sharding import PartitionSpec as P

NB = 4
BS = 64
BANDS = 3
NT = 512
RADIUS = 4
STEP = 0.5
MARK = 8
SHRINKAGE = 0.05
SOURCES = NB * BS
WIDE = NB * 2 * BS
MIB = 1 << 20
VMEM = pl.BlockSpec(memory_space=pltpu.VMEM)
ANY = pl.BlockSpec(memory_space=pl.ANY)


def split_table(freq_count):
    phases = np.arange(NT)[:, None] * (np.arange(freq_count) + 1)[None, :] % NT
    angles = phases * (2.0 * math.pi / NT)
    table = np.stack([np.cos(angles), -np.sin(angles)], axis=-1).reshape(NT, 2 * freq_count) / math.sqrt(NT)
    table = table.T.astype(np.float32)
    upper = table.astype(jnp.bfloat16)
    lower = (table - upper.astype(np.float32)).astype(jnp.bfloat16)
    return np.concatenate([upper, lower], axis=0)


def contract(a, b, dims):
    return lax.dot_general(a, b, ((dims[:1], dims[1:]), ((), ())), preferred_element_type=jnp.float32)


def clamp(u):
    return jnp.clip(u, -SHRINKAGE, SHRINKAGE)


def params(limit):
    return pltpu.CompilerParams(vmem_limit_bytes=limit * MIB)


def chunk_rows(rows, most):
    return max(size for size in range(128, most + 1, 128) if rows % size == 0)


def chunks(rows):
    unit = rows // 128 // 6 * 128
    bounds = [0, unit, 2 * unit, 4 * unit, rows] if unit else [0, rows]
    return [slice(low, high) for low, high in zip(bounds[:-1], bounds[1:])]


def build_operator(index_ref, multiples_ref, operator_ref):
    operator_ref[...] = jnp.zeros_like(operator_ref)
    for block in range(NB):
        columns = slice(block * 2 * BS, (block + 1) * 2 * BS)
        for band in range(BANDS):
            first = pl.multiple_of(index_ref[block, band] * BS, BS)
            pair = multiples_ref[block, band]
            operator_ref[pl.ds(first, BS), columns] = pair
            operator_ref[pl.ds(SOURCES + first, BS), columns] = jnp.concatenate([-pair[:, BS:], pair[:, :BS]], axis=1)


def forward_kernel(
    field_hbm, table_hbm, index_hbm, multiples_hbm, recorded_hbm, radius_hbm,
    narrow_ref, spectra_ref, field_ref, table_ref, operator_ref, recorded_ref, radius_ref,
    index, multiples, loaded, unpacked, radius, sems, field_sems,
):
    receivers = recorded_ref.shape[0]
    count, rows = spectra_ref.shape
    parts = chunks(rows)
    small = [
        pltpu.make_async_copy(table_hbm, table_ref, sems.at[0]),
        pltpu.make_async_copy(index_hbm, index, sems.at[1]),
        pltpu.make_async_copy(multiples_hbm, multiples, sems.at[2]),
        pltpu.make_async_copy(recorded_hbm, loaded, sems.at[3]),
        pltpu.make_async_copy(radius_hbm, radius, sems.at[4]),
    ]
    large = []
    for i, part in enumerate(parts):
        place = pl.ds(part.start, part.stop - part.start)
        large.append(pltpu.make_async_copy(field_hbm.at[place], field_ref.at[place], field_sems.at[i]))
    for copy in small[:1] + large[:2] + small[1:] + large[2:]:
        copy.start()

    def transform(i):
        large[i].wait()
        both = contract(table_ref[...], field_ref[parts[i]], (1, 1))
        spectra = both[:count] + both[count:]
        spectra_ref[:, parts[i]] = spectra
        narrow_ref[:, parts[i]] = spectra.astype(jnp.bfloat16)

    small[0].wait()
    transform(0)
    small[1].wait()
    small[2].wait()
    build_operator(index, multiples, operator_ref)
    for i in range(1, len(parts) // 2):
        transform(i)
    small[3].wait()
    unpacked[...] = loaded[...].astype(jnp.float32)
    for block in range(NB):
        recorded_ref[:, block * 2 * BS : (block + 1) * 2 * BS] = unpacked[pl.ds(block, receivers, stride=NB), :]
    small[4].wait()
    radius_ref[...] = radius[...].astype(jnp.float32).astype(jnp.bfloat16)
    for i in range(max(1, len(parts) // 2), len(parts)):
        transform(i)


def forward(field, table, block_index, multiples, recorded, radius):
    rows, receivers = field.shape[0], radius.shape[1]
    count = table.shape[0] // 2
    arguments = (field, table, block_index, multiples, recorded, radius)
    return pl.pallas_call(
        forward_kernel,
        in_specs=[ANY] * 6,
        out_specs=[VMEM] * 7,
        out_shape=[
            jax.ShapeDtypeStruct((count, rows), jnp.bfloat16),
            pltpu.VMEM((count, rows), jnp.float32),
            pltpu.VMEM((rows, NT), jnp.bfloat16),
            pltpu.VMEM(table.shape, jnp.bfloat16),
            pltpu.VMEM((2 * SOURCES, WIDE), jnp.bfloat16),
            pltpu.VMEM((receivers, WIDE), jnp.float32),
            jax.ShapeDtypeStruct(radius.shape, jnp.bfloat16),
        ],
        scratch_shapes=[
            pltpu.SMEM((NB, BANDS), jnp.int32),
            pltpu.VMEM((NB, BANDS, BS, 2 * BS), jnp.bfloat16),
            pltpu.VMEM((receivers * NB, 2 * BS), jnp.bfloat16),
            pltpu.VMEM((receivers * NB, 2 * BS), jnp.float32),
            pltpu.VMEM(radius.shape, jnp.int32),
            pltpu.SemaphoreType.DMA((5,)),
            pltpu.SemaphoreType.DMA((len(chunks(rows)),)),
        ],
        compiler_params=params(16),
        name="forward_dft",
    )(*(pltpu.with_memory_space_constraint(a, pltpu.HBM) for a in arguments))


def gradient_of(returned_ref, table_ref, part):
    returned = returned_ref[:, part]
    return contract(jnp.concatenate([returned, returned], axis=0), table_ref[...], (0, 0))


def middle_kernel(start_ref, returned_ref, spectra_ref, table_ref, field_ref, narrow_ref, *, step):
    count, rows = spectra_ref.shape
    for i in range(rows // step):
        part = slice(i * step, (i + 1) * step)
        update = start_ref[part].astype(jnp.float32) + gradient_of(returned_ref, table_ref, part)
        clamped = clamp(update)
        field_ref[part] = update - clamped
        both = contract(table_ref[...], clamped.astype(jnp.bfloat16), (1, 1))
        linear = spectra_ref[:, part] + 0.5 * returned_ref[:, part].astype(jnp.float32)
        narrow_ref[:, part] = (linear - (both[:count] + both[count:])).astype(jnp.bfloat16)


def middle(start, returned, spectra, table):
    rows = start.shape[0]
    step = chunk_rows(rows, 768)
    return pl.pallas_call(
        lambda *refs: middle_kernel(*refs, step=step),
        in_specs=[VMEM] * 4,
        out_specs=[VMEM] * 2,
        out_shape=[pltpu.VMEM((rows, NT), jnp.float32), jax.ShapeDtypeStruct(spectra.shape, jnp.bfloat16)],
        compiler_params=params(16),
        name="update_and_forward",
    )(start, returned, spectra, table)


def final_kernel(field_ref, returned_ref, table_ref, out_hbm, buffer, sems):
    slots, step, _ = buffer.shape
    rows = field_ref.shape[0]
    copies = []
    for i in range(rows // step):
        if i >= slots:
            copies[i - slots].wait()
        part = slice(i * step, (i + 1) * step)
        update = field_ref[part] + gradient_of(returned_ref, table_ref, part)
        buffer[i % slots] = update - clamp(update)
        copies.append(
            pltpu.make_async_copy(buffer.at[i % slots], out_hbm.at[pl.ds(i * step, step)], sems.at[i % slots])
        )
        copies[i].start()
    for copy in copies[-slots:]:
        copy.wait()


def final(field, returned, table):
    rows = field.shape[0]
    step = chunk_rows(rows, 512)
    slots = min(4, rows // step)
    return pl.pallas_call(
        final_kernel,
        in_specs=[VMEM] * 3,
        out_specs=ANY,
        out_shape=pltpu.HBM((rows, NT), jnp.float32),
        scratch_shapes=[pltpu.VMEM((slots, step, NT), jnp.float32), pltpu.SemaphoreType.DMA((slots,))],
        compiler_params=params(16),
        name="last_update",
    )(field, returned, table)


def smooth(backward, radius):
    sources, receivers = radius.shape
    rows = jnp.concatenate([backward[:sources], backward[sources:]], axis=1)
    narrow = rows.astype(jnp.bfloat16)
    radius = jnp.concatenate([radius, radius], axis=1)
    distance = jnp.abs(
        lax.broadcasted_iota(jnp.int32, (sources, sources), 0) - lax.broadcasted_iota(jnp.int32, (sources, sources), 1)
    )
    summed = rows
    for width in range(1, RADIUS + 1):
        band = jnp.where(distance <= width, 1.0, 0.0).astype(jnp.bfloat16)
        summed = jnp.where(radius >= width, contract(band, narrow, (1, 0)), summed)
    smoothed = (summed * (STEP / (2.0 * radius + 1.0))).astype(jnp.bfloat16)
    return jnp.concatenate([smoothed[:, :receivers], smoothed[:, receivers:]], axis=0)


def adjoint(arrived_ref, operator_ref, recorded_ref):
    operator = operator_ref[...]
    residual = recorded_ref[...] - contract(arrived_ref[...], operator, (0, 0))
    return residual, contract(operator, residual.astype(jnp.bfloat16), (1, 1))


def first_owner_kernel(arrived_ref, operator_ref, recorded_ref, backward_ref):
    _, backward_ref[...] = adjoint(arrived_ref, operator_ref, recorded_ref)


def smooth_kernel(backward_ref, radius_ref, returned_ref):
    returned_ref[...] = smooth(backward_ref[...], radius_ref[...].astype(jnp.float32))


def last_owner_kernel(
    arrived_ref, operator_ref, recorded_ref, radius_ref, returned_ref, residual_hbm, interleaved, sem
):
    residual, backward = adjoint(arrived_ref, operator_ref, recorded_ref)
    for block in range(NB):
        rows = pl.ds(block, residual.shape[0], stride=NB)
        interleaved[rows, :] = residual[:, block * 2 * BS : (block + 1) * 2 * BS]
    copy = pltpu.make_async_copy(interleaved, residual_hbm, sem)
    copy.start()
    returned_ref[...] = smooth(backward, radius_ref[...].astype(jnp.float32))
    copy.wait()


def first_owner(arrived, operator, recorded):
    receivers = arrived.shape[1]
    return pl.pallas_call(
        first_owner_kernel,
        in_specs=[VMEM] * 3,
        out_specs=VMEM,
        out_shape=pltpu.VMEM((2 * SOURCES, receivers), jnp.float32),
        compiler_params=params(16),
        cost_estimate=pl.CostEstimate(
            flops=8 * receivers * SOURCES * WIDE, bytes_accessed=8 * receivers * WIDE, transcendentals=0
        ),
        name="owner_products",
    )(arrived, operator, recorded)


def smooth_sources(backward, radius):
    return pl.pallas_call(
        smooth_kernel,
        in_specs=[VMEM] * 2,
        out_specs=VMEM,
        out_shape=jax.ShapeDtypeStruct(backward.shape, jnp.bfloat16),
        compiler_params=params(16),
        name="smooth_sources",
    )(backward, radius)


def last_owner(arrived, operator, recorded, radius):
    receivers = arrived.shape[1]
    return pl.pallas_call(
        last_owner_kernel,
        in_specs=[VMEM] * 4,
        out_specs=[VMEM, ANY],
        out_shape=[
            jax.ShapeDtypeStruct((2 * SOURCES, receivers), jnp.bfloat16),
            pltpu.HBM((receivers * NB, 2 * BS), jnp.float32),
        ],
        scratch_shapes=[pltpu.VMEM((receivers * NB, 2 * BS), jnp.float32), pltpu.SemaphoreType.DMA(())],
        compiler_params=params(16),
        name="owner_step",
    )(arrived, operator, recorded, radius)


def exchange(pieces):
    return lax.all_to_all(pieces, "freq", split_axis=0, concat_axis=0, tiled=True)


def on_device(start_field, recorded, multiples, block_index, radius):
    devices = lax.axis_size("freq")
    local_src, receivers, _ = start_field.shape
    rows = local_src * receivers
    table = jnp.asarray(split_table(devices))

    def by_part(arrived):
        return arrived.reshape(devices, 2, local_src, receivers).swapaxes(0, 1).reshape(2 * SOURCES, receivers)

    def to_owners(narrow):
        return by_part(exchange(narrow.reshape(devices, 2, local_src, receivers)))

    def to_owners_with_radius(narrow, radius):
        shares = 2 if devices % 2 == 0 and local_src % 2 == 0 else 1
        rows = local_src // shares
        marked = radius.reshape(shares, rows, receivers) + MARK * jnp.arange(shares, dtype=radius.dtype)[:, None, None]
        marked = jnp.broadcast_to(marked, (devices // shares, shares, rows, receivers))
        narrow = lax.optimization_barrier(narrow.reshape(devices, 2, local_src, receivers))
        pieces = [
            narrow.reshape(devices, 2 * shares, rows, receivers),
            marked.reshape(devices, 1, rows, receivers),
        ]
        arrived = exchange(jnp.concatenate(pieces, axis=1))
        halves = [arrived[:, 2 * shares]]
        if shares == 2:
            own, other = halves[0], lax.ppermute(halves[0], "freq", [(i, i ^ 1) for i in range(devices)])
            halves = [jnp.minimum(own, other), jnp.maximum(own, other) - MARK]
        return by_part(arrived[:, : 2 * shares]), jnp.stack(halves, axis=1).reshape(SOURCES, receivers)

    def to_traces(returned):
        pieces = returned.reshape(2, devices, local_src, receivers).swapaxes(0, 1)
        return exchange(pieces).reshape(2 * devices, rows)

    narrow, spectra, start, table, operator, recorded, radius = forward(
        start_field.reshape(rows, NT), table, block_index, multiples[0], recorded.reshape(-1, 2 * BS), radius
    )
    arrived, radius = to_owners_with_radius(narrow, radius)
    returned = smooth_sources(first_owner(arrived, operator, recorded), radius)
    field, narrow = middle(start, to_traces(returned), spectra, table)
    returned, residual = last_owner(to_owners(narrow), operator, recorded, radius)
    field = final(field, to_traces(returned), table)
    return field.reshape(local_src, receivers, NT), residual.reshape(1, receivers, NB, 2 * BS)


def solution(mesh):
    placed = (
        P(("grp", "freq"), None, None),
        P(("grp", "freq"), None, None, None),
        P(("grp", "freq"), None, None, None, None),
        P(),
        P(("grp", "freq"), None),
    )
    return jax.shard_map(
        on_device,
        mesh=mesh,
        in_specs=placed,
        out_specs=(P(("grp", "freq"), None, None), P(("grp", "freq"), None, None, None)),
        check_vma=False,
    )
```

```python
import math

import jax
import jax.numpy as jnp
import numpy as np
from jax import lax
from jax.experimental import pallas as pl
from jax.experimental.pallas import tpu as pltpu
from jax.sharding import PartitionSpec as P

NB = 4
BS = 64
BANDS = 3
NT = 512
RADIUS = 4
STEP = 0.5
MARK = 8
RANKS = (9, 11, 7, 3, 1, 4, 13, 8, 2, 5, 6, 12, 10, 0, 15, 14)
SHRINKAGE = 0.05
SOURCES = NB * BS
WIDE = NB * 2 * BS
MIB = 1 << 20
VMEM = pl.BlockSpec(memory_space=pltpu.VMEM)
ANY = pl.BlockSpec(memory_space=pl.ANY)


def ranking(devices, local_src):
    fits = devices == len(RANKS) and local_src % 16 == 0 and BS % local_src == 0
    return list(RANKS) if fits else list(range(devices))


def split_table(ranks):
    phases = np.arange(NT)[:, None] * (np.array(ranks) + 1)[None, :] % NT
    angles = phases * (2.0 * math.pi / NT)
    table = np.stack([np.cos(angles), -np.sin(angles)], axis=-1).reshape(NT, 2 * len(ranks)) / math.sqrt(NT)
    table = table.T.astype(np.float32)
    upper = table.astype(jnp.bfloat16)
    lower = (table - upper.astype(np.float32)).astype(jnp.bfloat16)
    return np.concatenate([upper, lower], axis=0)


def row_places(ranks):
    return np.arange(NB, dtype=np.int32) if ranks == sorted(ranks) else np.argsort(ranks).astype(np.int32)


def distances(ranks, local_src):
    sources = (np.array(ranks)[:, None] * local_src + np.arange(local_src)).reshape(-1)
    return np.abs(sources[:, None] - sources[None, :]).astype(np.float32)


def contract(a, b, dims):
    return lax.dot_general(a, b, ((dims[:1], dims[1:]), ((), ())), preferred_element_type=jnp.float32)


def clamp(u):
    return jnp.clip(u, -SHRINKAGE, SHRINKAGE)


def params(limit):
    return pltpu.CompilerParams(vmem_limit_bytes=limit * MIB)


def chunk_rows(rows, most):
    return max(size for size in range(128, most + 1, 128) if rows % size == 0)


def chunks(rows):
    unit = rows // 128 // 6 * 128
    bounds = [0, unit, 2 * unit, 4 * unit, rows] if unit else [0, rows]
    return [slice(low, high) for low, high in zip(bounds[:-1], bounds[1:])]


def build_operator(index_ref, places_ref, multiples_ref, operator_ref):
    operator_ref[...] = jnp.zeros_like(operator_ref)
    runs = places_ref.shape[0] // NB
    length = BS // runs
    for block in range(NB):
        columns = slice(block * 2 * BS, (block + 1) * 2 * BS)
        for band in range(BANDS):
            pair = multiples_ref[block, band]
            turned = jnp.concatenate([-pair[:, BS:], pair[:, :BS]], axis=1)
            for run in range(runs):
                first = pl.multiple_of(places_ref[index_ref[block, band] * runs + run] * length, length)
                part = slice(run * length, (run + 1) * length)
                operator_ref[pl.ds(first, length), columns] = pair[part]
                operator_ref[pl.ds(SOURCES + first, length), columns] = turned[part]


def forward_kernel(
    field_hbm, table_hbm, index_hbm, places_hbm, multiples_hbm, recorded_hbm, radius_hbm, distance_hbm,
    narrow_ref, spectra_ref, field_ref, table_ref, operator_ref, recorded_ref, radius_ref, distance_ref,
    index, places, multiples, loaded, unpacked, radius, sems, field_sems, *, halves,
):
    receivers = recorded_ref.shape[0]
    count, rows = spectra_ref.shape
    parts = chunks(rows)
    small = [
        pltpu.make_async_copy(table_hbm, table_ref, sems.at[0]),
        pltpu.make_async_copy(index_hbm, index, sems.at[1]),
        pltpu.make_async_copy(multiples_hbm, multiples, sems.at[2]),
        pltpu.make_async_copy(recorded_hbm, loaded, sems.at[3]),
        pltpu.make_async_copy(radius_hbm, radius, sems.at[4]),
        pltpu.make_async_copy(places_hbm, places, sems.at[5]),
        pltpu.make_async_copy(distance_hbm, distance_ref, sems.at[6]),
    ]
    large = []
    for i, part in enumerate(parts):
        place = pl.ds(part.start, part.stop - part.start)
        large.append(pltpu.make_async_copy(field_hbm.at[place], field_ref.at[place], field_sems.at[i]))
    for copy in small[:1] + large[:2] + small[1:] + large[2:]:
        copy.start()

    def transform(i):
        large[i].wait()
        both = contract(table_ref[...], field_ref[parts[i]], (1, 1))
        spectra = both[:count] + both[count:]
        spectra_ref[:, parts[i]] = spectra
        narrow_ref[:, parts[i]] = spectra.astype(jnp.bfloat16)

    small[0].wait()
    transform(0)
    small[1].wait()
    small[2].wait()
    small[5].wait()
    build_operator(index, places, multiples, operator_ref)
    for i in range(1, len(parts) // 2):
        transform(i)
    small[3].wait()
    unpacked[...] = loaded[...].astype(jnp.float32)
    for block in range(NB):
        recorded_ref[:, block * 2 * BS : (block + 1) * 2 * BS] = unpacked[pl.ds(block, receivers, stride=NB), :]
    small[4].wait()
    shares, amount = max(halves) + 1, radius_ref.shape[1]
    for share in range(shares):
        rows_sent = radius[share * amount : (share + 1) * amount].astype(jnp.float32) + MARK * share
        for rank, half in enumerate(halves):
            if half == share:
                radius_ref[rank] = rows_sent.astype(jnp.bfloat16)
    for i in range(max(1, len(parts) // 2), len(parts)):
        transform(i)
    small[6].wait()


def forward(field, table, block_index, places, multiples, recorded, radius, distance, halves):
    rows, receivers = field.shape[0], radius.shape[1]
    count = table.shape[0] // 2
    arguments = (field, table, block_index, places, multiples, recorded, radius, distance)
    sent = (len(halves), radius.shape[0] // (max(halves) + 1), receivers)
    return pl.pallas_call(
        lambda *refs: forward_kernel(*refs, halves=halves),
        in_specs=[ANY] * 8,
        out_specs=[VMEM] * 8,
        out_shape=[
            jax.ShapeDtypeStruct((count, rows), jnp.bfloat16),
            pltpu.VMEM((count, rows), jnp.float32),
            pltpu.VMEM((rows, NT), jnp.bfloat16),
            pltpu.VMEM(table.shape, jnp.bfloat16),
            pltpu.VMEM((2 * SOURCES, WIDE), jnp.bfloat16),
            pltpu.VMEM((receivers, WIDE), jnp.float32),
            jax.ShapeDtypeStruct(sent, jnp.bfloat16),
            pltpu.VMEM(distance.shape, jnp.float32),
        ],
        scratch_shapes=[
            pltpu.SMEM((NB, BANDS), jnp.int32),
            pltpu.SMEM(places.shape, jnp.int32),
            pltpu.VMEM((NB, BANDS, BS, 2 * BS), jnp.bfloat16),
            pltpu.VMEM((receivers * NB, 2 * BS), jnp.bfloat16),
            pltpu.VMEM((receivers * NB, 2 * BS), jnp.float32),
            pltpu.VMEM(radius.shape, jnp.int32),
            pltpu.SemaphoreType.DMA((7,)),
            pltpu.SemaphoreType.DMA((len(chunks(rows)),)),
        ],
        compiler_params=params(16),
        name="forward_dft",
    )(*(pltpu.with_memory_space_constraint(a, pltpu.HBM) for a in arguments))


def gradient_of(returned_ref, table_ref, part):
    returned = returned_ref[:, part]
    return contract(jnp.concatenate([returned, returned], axis=0), table_ref[...], (0, 0))


def middle_kernel(start_ref, returned_ref, spectra_ref, table_ref, field_ref, narrow_ref, *, step):
    count, rows = spectra_ref.shape
    for i in range(rows // step):
        part = slice(i * step, (i + 1) * step)
        update = start_ref[part].astype(jnp.float32) + gradient_of(returned_ref, table_ref, part)
        clamped = clamp(update)
        field_ref[part] = update - clamped
        both = contract(table_ref[...], clamped.astype(jnp.bfloat16), (1, 1))
        linear = spectra_ref[:, part] + 0.5 * returned_ref[:, part].astype(jnp.float32)
        narrow_ref[:, part] = (linear - (both[:count] + both[count:])).astype(jnp.bfloat16)


def middle(start, returned, spectra, table):
    rows = start.shape[0]
    step = chunk_rows(rows, 768)
    return pl.pallas_call(
        lambda *refs: middle_kernel(*refs, step=step),
        in_specs=[VMEM] * 4,
        out_specs=[VMEM] * 2,
        out_shape=[pltpu.VMEM((rows, NT), jnp.float32), jax.ShapeDtypeStruct(spectra.shape, jnp.bfloat16)],
        compiler_params=params(16),
        name="update_and_forward",
    )(start, returned, spectra, table)


def final_kernel(field_ref, returned_ref, table_ref, out_hbm, buffer, sems):
    slots, step, _ = buffer.shape
    rows = field_ref.shape[0]
    copies = []
    for i in range(rows // step):
        if i >= slots:
            copies[i - slots].wait()
        part = slice(i * step, (i + 1) * step)
        update = field_ref[part] + gradient_of(returned_ref, table_ref, part)
        buffer[i % slots] = update - clamp(update)
        copies.append(
            pltpu.make_async_copy(buffer.at[i % slots], out_hbm.at[pl.ds(i * step, step)], sems.at[i % slots])
        )
        copies[i].start()
    for copy in copies[-slots:]:
        copy.wait()


def final(field, returned, table):
    rows = field.shape[0]
    step = chunk_rows(rows, 512)
    slots = min(4, rows // step)
    return pl.pallas_call(
        final_kernel,
        in_specs=[VMEM] * 3,
        out_specs=ANY,
        out_shape=pltpu.HBM((rows, NT), jnp.float32),
        scratch_shapes=[pltpu.VMEM((slots, step, NT), jnp.float32), pltpu.SemaphoreType.DMA((slots,))],
        compiler_params=params(16),
        name="last_update",
    )(field, returned, table)


def smooth(backward, radius, distance):
    sources, receivers = radius.shape
    rows = jnp.concatenate([backward[:sources], backward[sources:]], axis=1)
    narrow = rows.astype(jnp.bfloat16)
    radius = jnp.concatenate([radius, radius], axis=1)
    summed = rows
    for width in range(1, RADIUS + 1):
        band = jnp.where(distance <= width, 1.0, 0.0).astype(jnp.bfloat16)
        summed = jnp.where(radius >= width, contract(band, narrow, (1, 0)), summed)
    smoothed = (summed * (STEP / (2.0 * radius + 1.0))).astype(jnp.bfloat16)
    return jnp.concatenate([smoothed[:, :receivers], smoothed[:, receivers:]], axis=0)


def adjoint(arrived_ref, operator_ref, recorded_ref):
    operator = operator_ref[...]
    residual = recorded_ref[...] - contract(arrived_ref[...], operator, (0, 0))
    return residual, contract(operator, residual.astype(jnp.bfloat16), (1, 1))


def first_owner_kernel(arrived_ref, operator_ref, recorded_ref, backward_ref):
    _, backward_ref[...] = adjoint(arrived_ref, operator_ref, recorded_ref)


def smooth_kernel(backward_ref, radius_ref, distance_ref, returned_ref):
    returned_ref[...] = smooth(backward_ref[...], radius_ref[...].astype(jnp.float32), distance_ref[...])


def last_owner_kernel(
    arrived_ref, operator_ref, recorded_ref, radius_ref, distance_ref, returned_ref, residual_hbm, interleaved, sem
):
    residual, backward = adjoint(arrived_ref, operator_ref, recorded_ref)
    for block in range(NB):
        rows = pl.ds(block, residual.shape[0], stride=NB)
        interleaved[rows, :] = residual[:, block * 2 * BS : (block + 1) * 2 * BS]
    copy = pltpu.make_async_copy(interleaved, residual_hbm, sem)
    copy.start()
    returned_ref[...] = smooth(backward, radius_ref[...].astype(jnp.float32), distance_ref[...])
    copy.wait()


def first_owner(arrived, operator, recorded):
    receivers = arrived.shape[1]
    return pl.pallas_call(
        first_owner_kernel,
        in_specs=[VMEM] * 3,
        out_specs=VMEM,
        out_shape=pltpu.VMEM((2 * SOURCES, receivers), jnp.float32),
        compiler_params=params(16),
        cost_estimate=pl.CostEstimate(
            flops=8 * receivers * SOURCES * WIDE, bytes_accessed=8 * receivers * WIDE, transcendentals=0
        ),
        name="owner_products",
    )(arrived, operator, recorded)


def smooth_sources(backward, radius, distance):
    return pl.pallas_call(
        smooth_kernel,
        in_specs=[VMEM] * 3,
        out_specs=VMEM,
        out_shape=jax.ShapeDtypeStruct(backward.shape, jnp.bfloat16),
        compiler_params=params(16),
        name="smooth_sources",
    )(backward, radius, distance)


def last_owner(arrived, operator, recorded, radius, distance):
    receivers = arrived.shape[1]
    return pl.pallas_call(
        last_owner_kernel,
        in_specs=[VMEM] * 5,
        out_specs=[VMEM, ANY],
        out_shape=[
            jax.ShapeDtypeStruct((2 * SOURCES, receivers), jnp.bfloat16),
            pltpu.HBM((receivers * NB, 2 * BS), jnp.float32),
        ],
        scratch_shapes=[pltpu.VMEM((receivers * NB, 2 * BS), jnp.float32), pltpu.SemaphoreType.DMA(())],
        compiler_params=params(16),
        name="owner_step",
    )(arrived, operator, recorded, radius, distance)


def on_device(start_field, recorded, multiples, block_index, radius):
    devices = lax.axis_size("freq")
    local_src, receivers, _ = start_field.shape
    rows = local_src * receivers
    ranks = ranking(devices, local_src)
    places = row_places(ranks)
    shares = 2 if devices % 2 == 0 and local_src % 2 == 0 else 1
    table = jnp.asarray(split_table(ranks))

    def exchange(pieces):
        return lax.all_to_all(pieces, "freq", split_axis=0, concat_axis=0, tiled=True, axis_index_groups=[ranks])

    def by_part(arrived):
        return arrived.reshape(devices, 2, local_src, receivers).swapaxes(0, 1).reshape(2 * SOURCES, receivers)

    def to_owners(narrow):
        return by_part(exchange(narrow.reshape(devices, 2, local_src, receivers)))

    def to_owners_with_radius(narrow, radius):
        rows = local_src // shares
        narrow = lax.optimization_barrier(narrow.reshape(devices, 2, local_src, receivers))
        pieces = [
            narrow.reshape(devices, 2 * shares, rows, receivers),
            radius.reshape(devices, 1, rows, receivers),
        ]
        arrived = exchange(jnp.concatenate(pieces, axis=1))
        halves = [arrived[:, 2 * shares]]
        if shares == 2:
            own, other = halves[0], lax.ppermute(halves[0], "freq", [(i, i ^ 1) for i in range(devices)])
            halves = [jnp.minimum(own, other), jnp.maximum(own, other) - MARK]
        return by_part(arrived[:, : 2 * shares]), jnp.stack(halves, axis=1).reshape(SOURCES, receivers)

    def to_traces(returned):
        pieces = returned.reshape(2, devices, local_src, receivers).swapaxes(0, 1)
        return exchange(pieces).reshape(2 * devices, rows)

    narrow, spectra, start, table, operator, recorded, radius, distance = forward(
        start_field.reshape(rows, NT),
        table,
        block_index,
        jnp.asarray(places),
        multiples[0],
        recorded.reshape(-1, 2 * BS),
        radius,
        jnp.asarray(distances(ranks, local_src)),
        [rank % shares for rank in ranks],
    )
    arrived, radius = to_owners_with_radius(narrow, radius)
    returned = smooth_sources(first_owner(arrived, operator, recorded), radius, distance)
    field, narrow = middle(start, to_traces(returned), spectra, table)
    returned, residual = last_owner(to_owners(narrow), operator, recorded, radius, distance)
    field = final(field, to_traces(returned), table)
    return field.reshape(local_src, receivers, NT), residual.reshape(1, receivers, NB, 2 * BS)


def solution(mesh):
    placed = (
        P(("grp", "freq"), None, None),
        P(("grp", "freq"), None, None, None),
        P(("grp", "freq"), None, None, None, None),
        P(),
        P(("grp", "freq"), None),
    )
    return jax.shard_map(
        on_device,
        mesh=mesh,
        in_specs=placed,
        out_specs=(P(("grp", "freq"), None, None), P(("grp", "freq"), None, None, None)),
        check_vma=False,
    )
```

```python
import math

import jax
import jax.numpy as jnp
import numpy as np
from jax import lax
from jax.experimental import pallas as pl
from jax.experimental.pallas import tpu as pltpu
from jax.sharding import PartitionSpec as P

NB = 4
BS = 64
BANDS = 3
NT = 512
RADIUS = 4
STEP = 0.5
MARK = 8
RANKS = (11, 13, 15, 1, 3, 6, 5, 9, 2, 7, 4, 14, 8, 12, 10, 0)
SHRINKAGE = 0.05
SOURCES = NB * BS
WIDE = NB * 2 * BS
MIB = 1 << 20
VMEM = pl.BlockSpec(memory_space=pltpu.VMEM)
ANY = pl.BlockSpec(memory_space=pl.ANY)


def ranking(devices, local_src):
    fits = devices == len(RANKS) and local_src % 16 == 0 and BS % local_src == 0
    return list(RANKS) if fits else list(range(devices))


def split_table(ranks):
    phases = np.arange(NT)[:, None] * (np.array(ranks) + 1)[None, :] % NT
    angles = phases * (2.0 * math.pi / NT)
    table = np.stack([np.cos(angles), -np.sin(angles)], axis=-1).reshape(NT, 2 * len(ranks)) / math.sqrt(NT)
    table = table.T.astype(np.float32)
    upper = table.astype(jnp.bfloat16)
    lower = (table - upper.astype(np.float32)).astype(jnp.bfloat16)
    return np.concatenate([upper, lower], axis=0)


def row_places(ranks):
    return np.arange(NB, dtype=np.int32) if ranks == sorted(ranks) else np.argsort(ranks).astype(np.int32)


def distances(ranks, local_src):
    sources = (np.array(ranks)[:, None] * local_src + np.arange(local_src)).reshape(-1)
    return np.abs(sources[:, None] - sources[None, :]).astype(np.float32)


def contract(a, b, dims):
    return lax.dot_general(a, b, ((dims[:1], dims[1:]), ((), ())), preferred_element_type=jnp.float32)


def clamp(u):
    return jnp.clip(u, -SHRINKAGE, SHRINKAGE)


def params(limit):
    return pltpu.CompilerParams(vmem_limit_bytes=limit * MIB)


def chunk_rows(rows, most):
    return max(size for size in range(128, most + 1, 128) if rows % size == 0)


def chunks(rows):
    unit = rows // 128 // 6 * 128
    bounds = [0, unit, 2 * unit, 4 * unit, rows] if unit else [0, rows]
    return [slice(low, high) for low, high in zip(bounds[:-1], bounds[1:])]


def build_operator(index_ref, places_ref, multiples_ref, operator_ref):
    operator_ref[...] = jnp.zeros_like(operator_ref)
    runs = places_ref.shape[0] // NB
    length = BS // runs
    for block in range(NB):
        columns = slice(block * 2 * BS, (block + 1) * 2 * BS)
        for band in range(BANDS):
            pair = multiples_ref[block, band]
            turned = jnp.concatenate([-pair[:, BS:], pair[:, :BS]], axis=1)
            for run in range(runs):
                first = pl.multiple_of(places_ref[index_ref[block, band] * runs + run] * length, length)
                part = slice(run * length, (run + 1) * length)
                operator_ref[pl.ds(first, length), columns] = pair[part]
                operator_ref[pl.ds(SOURCES + first, length), columns] = turned[part]


def forward_kernel(
    field_hbm, table_hbm, index_hbm, places_hbm, multiples_hbm, recorded_hbm, radius_hbm, distance_hbm,
    narrow_ref, spectra_ref, field_ref, table_ref, operator_ref, recorded_ref, radius_ref, distance_ref,
    index, places, multiples, loaded, unpacked, radius, sems, field_sems, *, halves,
):
    receivers = recorded_ref.shape[0]
    count, rows = spectra_ref.shape
    parts = chunks(rows)
    small = [
        pltpu.make_async_copy(table_hbm, table_ref, sems.at[0]),
        pltpu.make_async_copy(index_hbm, index, sems.at[1]),
        pltpu.make_async_copy(multiples_hbm, multiples, sems.at[2]),
        pltpu.make_async_copy(recorded_hbm, loaded, sems.at[3]),
        pltpu.make_async_copy(radius_hbm, radius, sems.at[4]),
        pltpu.make_async_copy(places_hbm, places, sems.at[5]),
        pltpu.make_async_copy(distance_hbm, distance_ref, sems.at[6]),
    ]
    large = []
    for i, part in enumerate(parts):
        place = pl.ds(part.start, part.stop - part.start)
        large.append(pltpu.make_async_copy(field_hbm.at[place], field_ref.at[place], field_sems.at[i]))
    for copy in small[:1] + large[:2] + small[1:] + large[2:]:
        copy.start()

    def transform(i):
        large[i].wait()
        both = contract(table_ref[...], field_ref[parts[i]], (1, 1))
        spectra = both[:count] + both[count:]
        spectra_ref[:, parts[i]] = spectra
        narrow_ref[:, parts[i]] = spectra.astype(jnp.bfloat16)

    small[0].wait()
    transform(0)
    small[1].wait()
    small[2].wait()
    small[5].wait()
    build_operator(index, places, multiples, operator_ref)
    for i in range(1, len(parts) // 2):
        transform(i)
    small[3].wait()
    unpacked[...] = loaded[...].astype(jnp.float32)
    for block in range(NB):
        recorded_ref[:, block * 2 * BS : (block + 1) * 2 * BS] = unpacked[pl.ds(block, receivers, stride=NB), :]
    small[4].wait()
    shares, amount = max(halves) + 1, radius_ref.shape[1]
    for share in range(shares):
        rows_sent = radius[share * amount : (share + 1) * amount].astype(jnp.float32) + MARK * share
        for rank, half in enumerate(halves):
            if half == share:
                radius_ref[rank] = rows_sent.astype(jnp.bfloat16)
    for i in range(max(1, len(parts) // 2), len(parts)):
        transform(i)
    small[6].wait()


def forward(field, table, block_index, places, multiples, recorded, radius, distance, halves):
    rows, receivers = field.shape[0], radius.shape[1]
    count = table.shape[0] // 2
    arguments = (field, table, block_index, places, multiples, recorded, radius, distance)
    sent = (len(halves), radius.shape[0] // (max(halves) + 1), receivers)
    return pl.pallas_call(
        lambda *refs: forward_kernel(*refs, halves=halves),
        in_specs=[ANY] * 8,
        out_specs=[VMEM] * 8,
        out_shape=[
            jax.ShapeDtypeStruct((count, rows), jnp.bfloat16),
            pltpu.VMEM((count, rows), jnp.float32),
            pltpu.VMEM((rows, NT), jnp.bfloat16),
            pltpu.VMEM(table.shape, jnp.bfloat16),
            pltpu.VMEM((2 * SOURCES, WIDE), jnp.bfloat16),
            pltpu.VMEM((receivers, WIDE), jnp.float32),
            jax.ShapeDtypeStruct(sent, jnp.bfloat16),
            pltpu.VMEM(distance.shape, jnp.float32),
        ],
        scratch_shapes=[
            pltpu.SMEM((NB, BANDS), jnp.int32),
            pltpu.SMEM(places.shape, jnp.int32),
            pltpu.VMEM((NB, BANDS, BS, 2 * BS), jnp.bfloat16),
            pltpu.VMEM((receivers * NB, 2 * BS), jnp.bfloat16),
            pltpu.VMEM((receivers * NB, 2 * BS), jnp.float32),
            pltpu.VMEM(radius.shape, jnp.int32),
            pltpu.SemaphoreType.DMA((7,)),
            pltpu.SemaphoreType.DMA((len(chunks(rows)),)),
        ],
        compiler_params=params(16),
        name="forward_dft",
    )(*(pltpu.with_memory_space_constraint(a, pltpu.HBM) for a in arguments))


def gradient_of(returned_ref, table_ref, part):
    returned = returned_ref[:, part]
    return contract(jnp.concatenate([returned, returned], axis=0), table_ref[...], (0, 0))


def middle_kernel(start_ref, returned_ref, spectra_ref, table_ref, field_ref, narrow_ref, *, step):
    count, rows = spectra_ref.shape
    for i in range(rows // step):
        part = slice(i * step, (i + 1) * step)
        update = start_ref[part].astype(jnp.float32) + gradient_of(returned_ref, table_ref, part)
        clamped = clamp(update)
        field_ref[part] = update - clamped
        both = contract(table_ref[...], clamped.astype(jnp.bfloat16), (1, 1))
        linear = spectra_ref[:, part] + 0.5 * returned_ref[:, part].astype(jnp.float32)
        narrow_ref[:, part] = (linear - (both[:count] + both[count:])).astype(jnp.bfloat16)


def middle(start, returned, spectra, table):
    rows = start.shape[0]
    step = chunk_rows(rows, 768)
    return pl.pallas_call(
        lambda *refs: middle_kernel(*refs, step=step),
        in_specs=[VMEM] * 4,
        out_specs=[VMEM] * 2,
        out_shape=[pltpu.VMEM((rows, NT), jnp.float32), jax.ShapeDtypeStruct(spectra.shape, jnp.bfloat16)],
        compiler_params=params(16),
        name="update_and_forward",
    )(start, returned, spectra, table)


def final_kernel(field_ref, returned_ref, table_ref, out_hbm, buffer, sems):
    slots, step, _ = buffer.shape
    rows = field_ref.shape[0]
    copies = []
    for i in range(rows // step):
        if i >= slots:
            copies[i - slots].wait()
        part = slice(i * step, (i + 1) * step)
        update = field_ref[part] + gradient_of(returned_ref, table_ref, part)
        buffer[i % slots] = update - clamp(update)
        copies.append(
            pltpu.make_async_copy(buffer.at[i % slots], out_hbm.at[pl.ds(i * step, step)], sems.at[i % slots])
        )
        copies[i].start()
    for copy in copies[-slots:]:
        copy.wait()


def final(field, returned, table):
    rows = field.shape[0]
    step = chunk_rows(rows, 512)
    slots = min(4, rows // step)
    return pl.pallas_call(
        final_kernel,
        in_specs=[VMEM] * 3,
        out_specs=ANY,
        out_shape=pltpu.HBM((rows, NT), jnp.float32),
        scratch_shapes=[pltpu.VMEM((slots, step, NT), jnp.float32), pltpu.SemaphoreType.DMA((slots,))],
        compiler_params=params(16),
        name="last_update",
    )(field, returned, table)


def smooth(backward, radius, distance):
    sources, receivers = radius.shape
    rows = jnp.concatenate([backward[:sources], backward[sources:]], axis=1)
    narrow = rows.astype(jnp.bfloat16)
    radius = jnp.concatenate([radius, radius], axis=1)
    summed = rows
    for width in range(1, RADIUS + 1):
        band = jnp.where(distance <= width, 1.0, 0.0).astype(jnp.bfloat16)
        summed = jnp.where(radius >= width, contract(band, narrow, (1, 0)), summed)
    smoothed = (summed * (STEP / (2.0 * radius + 1.0))).astype(jnp.bfloat16)
    return jnp.concatenate([smoothed[:, :receivers], smoothed[:, receivers:]], axis=0)


def adjoint(arrived_ref, operator_ref, recorded_ref):
    operator = operator_ref[...]
    residual = recorded_ref[...] - contract(arrived_ref[...], operator, (0, 0))
    return residual, contract(operator, residual.astype(jnp.bfloat16), (1, 1))


def first_owner_kernel(arrived_ref, operator_ref, recorded_ref, backward_ref):
    _, backward_ref[...] = adjoint(arrived_ref, operator_ref, recorded_ref)


def smooth_kernel(backward_ref, radius_ref, distance_ref, returned_ref):
    returned_ref[...] = smooth(backward_ref[...], radius_ref[...].astype(jnp.float32), distance_ref[...])


def last_owner_kernel(
    arrived_ref, operator_ref, recorded_ref, radius_ref, distance_ref, returned_ref, residual_hbm, interleaved, sem
):
    residual, backward = adjoint(arrived_ref, operator_ref, recorded_ref)
    for block in range(NB):
        rows = pl.ds(block, residual.shape[0], stride=NB)
        interleaved[rows, :] = residual[:, block * 2 * BS : (block + 1) * 2 * BS]
    copy = pltpu.make_async_copy(interleaved, residual_hbm, sem)
    copy.start()
    returned_ref[...] = smooth(backward, radius_ref[...].astype(jnp.float32), distance_ref[...])
    copy.wait()


def first_owner(arrived, operator, recorded):
    receivers = arrived.shape[1]
    return pl.pallas_call(
        first_owner_kernel,
        in_specs=[VMEM] * 3,
        out_specs=VMEM,
        out_shape=pltpu.VMEM((2 * SOURCES, receivers), jnp.float32),
        compiler_params=params(16),
        cost_estimate=pl.CostEstimate(
            flops=8 * receivers * SOURCES * WIDE, bytes_accessed=8 * receivers * WIDE, transcendentals=0
        ),
        name="owner_products",
    )(arrived, operator, recorded)


def smooth_sources(backward, radius, distance):
    return pl.pallas_call(
        smooth_kernel,
        in_specs=[VMEM] * 3,
        out_specs=VMEM,
        out_shape=jax.ShapeDtypeStruct(backward.shape, jnp.bfloat16),
        compiler_params=params(16),
        name="smooth_sources",
    )(backward, radius, distance)


def last_owner(arrived, operator, recorded, radius, distance):
    receivers = arrived.shape[1]
    return pl.pallas_call(
        last_owner_kernel,
        in_specs=[VMEM] * 5,
        out_specs=[VMEM, ANY],
        out_shape=[
            jax.ShapeDtypeStruct((2 * SOURCES, receivers), jnp.bfloat16),
            pltpu.HBM((receivers * NB, 2 * BS), jnp.float32),
        ],
        scratch_shapes=[pltpu.VMEM((receivers * NB, 2 * BS), jnp.float32), pltpu.SemaphoreType.DMA(())],
        compiler_params=params(16),
        name="owner_step",
    )(arrived, operator, recorded, radius, distance)


def on_device(start_field, recorded, multiples, block_index, radius):
    devices = lax.axis_size("freq")
    local_src, receivers, _ = start_field.shape
    rows = local_src * receivers
    ranks = ranking(devices, local_src)
    places = row_places(ranks)
    shares = 2 if devices % 2 == 0 and local_src % 2 == 0 else 1
    table = jnp.asarray(split_table(ranks))

    def exchange(pieces):
        return lax.all_to_all(pieces, "freq", split_axis=0, concat_axis=0, tiled=True, axis_index_groups=[ranks])

    def by_part(arrived):
        return arrived.reshape(devices, 2, local_src, receivers).swapaxes(0, 1).reshape(2 * SOURCES, receivers)

    def to_owners(narrow):
        return by_part(exchange(narrow.reshape(devices, 2, local_src, receivers)))

    def to_owners_with_radius(narrow, radius):
        rows = local_src // shares
        narrow = lax.optimization_barrier(narrow.reshape(devices, 2, local_src, receivers))
        pieces = [
            narrow.reshape(devices, 2 * shares, rows, receivers),
            radius.reshape(devices, 1, rows, receivers),
        ]
        arrived = exchange(jnp.concatenate(pieces, axis=1))
        halves = [arrived[:, 2 * shares]]
        if shares == 2:
            own, other = halves[0], lax.ppermute(halves[0], "freq", [(i, i ^ 1) for i in range(devices)])
            halves = [jnp.minimum(own, other), jnp.maximum(own, other) - MARK]
        return by_part(arrived[:, : 2 * shares]), jnp.stack(halves, axis=1).reshape(SOURCES, receivers)

    def to_traces(returned):
        pieces = returned.reshape(2, devices, local_src, receivers).swapaxes(0, 1)
        return exchange(pieces).reshape(2 * devices, rows)

    narrow, spectra, start, table, operator, recorded, radius, distance = forward(
        start_field.reshape(rows, NT),
        table,
        block_index,
        jnp.asarray(places),
        multiples[0],
        recorded.reshape(-1, 2 * BS),
        radius,
        jnp.asarray(distances(ranks, local_src)),
        [rank % shares for rank in ranks],
    )
    arrived, radius = to_owners_with_radius(narrow, radius)
    returned = smooth_sources(first_owner(arrived, operator, recorded), radius, distance)
    field, narrow = middle(start, to_traces(returned), spectra, table)
    returned, residual = last_owner(to_owners(narrow), operator, recorded, radius, distance)
    field = final(field, to_traces(returned), table)
    return field.reshape(local_src, receivers, NT), residual.reshape(1, receivers, NB, 2 * BS)


def solution(mesh):
    placed = (
        P(("grp", "freq"), None, None),
        P(("grp", "freq"), None, None, None),
        P(("grp", "freq"), None, None, None, None),
        P(),
        P(("grp", "freq"), None),
    )
    return jax.shard_map(
        on_device,
        mesh=mesh,
        in_specs=placed,
        out_specs=(P(("grp", "freq"), None, None), P(("grp", "freq"), None, None, None)),
        check_vma=False,
    )
```

```python
import math

import jax
import jax.numpy as jnp
import numpy as np
from jax import lax
from jax.experimental import pallas as pl
from jax.experimental.pallas import tpu as pltpu
from jax.sharding import PartitionSpec as P

NB = 4
BS = 64
BANDS = 3
NT = 512
RADIUS = 4
STEP = 0.5
MARK = 8
RANKS = (11, 13, 15, 1, 3, 6, 5, 9, 2, 7, 4, 14, 8, 12, 10, 0)
SHRINKAGE = 0.05
SOURCES = NB * BS
WIDE = NB * 2 * BS
MIB = 1 << 20
VMEM = pl.BlockSpec(memory_space=pltpu.VMEM)
ANY = pl.BlockSpec(memory_space=pl.ANY)


def ranking(devices, local_src):
    fits = devices == len(RANKS) and local_src % 16 == 0 and BS % local_src == 0
    return list(RANKS) if fits else list(range(devices))


def split_table(ranks):
    phases = np.arange(NT)[:, None] * (np.array(ranks) + 1)[None, :] % NT
    angles = phases * (2.0 * math.pi / NT)
    table = np.stack([np.cos(angles), -np.sin(angles)], axis=-1).reshape(NT, 2 * len(ranks)) / math.sqrt(NT)
    table = table.T.astype(np.float32)
    upper = table.astype(jnp.bfloat16)
    lower = (table - upper.astype(np.float32)).astype(jnp.bfloat16)
    return np.concatenate([upper, lower], axis=0)


def row_places(ranks):
    return np.arange(NB, dtype=np.int32) if ranks == sorted(ranks) else np.argsort(ranks).astype(np.int32)


def distances(ranks, local_src):
    sources = (np.array(ranks)[:, None] * local_src + np.arange(local_src)).reshape(-1)
    return np.abs(sources[:, None] - sources[None, :]).astype(np.float32)


def contract(a, b, dims):
    return lax.dot_general(a, b, ((dims[:1], dims[1:]), ((), ())), preferred_element_type=jnp.float32)


def clamp(u):
    return jnp.clip(u, -SHRINKAGE, SHRINKAGE)


def params(limit):
    return pltpu.CompilerParams(vmem_limit_bytes=limit * MIB)


def chunk_rows(rows, most):
    return max(size for size in range(128, most + 1, 128) if rows % size == 0)


def chunks(rows):
    unit = rows // 128 // 6 * 128
    bounds = [0, unit, 2 * unit, 4 * unit, rows] if unit else [0, rows]
    return [slice(low, high) for low, high in zip(bounds[:-1], bounds[1:])]


def build_operator(index_ref, places_ref, multiples_ref, operator_ref):
    operator_ref[...] = jnp.zeros_like(operator_ref)
    runs = places_ref.shape[0] // NB
    length = BS // runs
    for block in range(NB):
        columns = slice(block * 2 * BS, (block + 1) * 2 * BS)
        for band in range(BANDS):
            pair = multiples_ref[block, band]
            turned = jnp.concatenate([-pair[:, BS:], pair[:, :BS]], axis=1)
            for run in range(runs):
                first = pl.multiple_of(places_ref[index_ref[block, band] * runs + run] * length, length)
                part = slice(run * length, (run + 1) * length)
                operator_ref[pl.ds(first, length), columns] = pair[part]
                operator_ref[pl.ds(SOURCES + first, length), columns] = turned[part]


def forward_kernel(
    field_hbm, table_hbm, index_hbm, places_hbm, multiples_hbm, recorded_hbm, radius_hbm, distance_hbm,
    narrow_ref, spectra_ref, field_ref, table_ref, operator_ref, recorded_ref, radius_ref, distance_ref,
    index, places, multiples, loaded, unpacked, radius, sems, field_sems, *, halves,
):
    receivers = recorded_ref.shape[0]
    count, rows = spectra_ref.shape
    parts = chunks(rows)
    small = [
        pltpu.make_async_copy(table_hbm, table_ref, sems.at[0]),
        pltpu.make_async_copy(index_hbm, index, sems.at[1]),
        pltpu.make_async_copy(multiples_hbm, multiples, sems.at[2]),
        pltpu.make_async_copy(recorded_hbm, loaded, sems.at[3]),
        pltpu.make_async_copy(radius_hbm, radius, sems.at[4]),
        pltpu.make_async_copy(places_hbm, places, sems.at[5]),
        pltpu.make_async_copy(distance_hbm, distance_ref, sems.at[6]),
    ]
    large = []
    for i, part in enumerate(parts):
        place = pl.ds(part.start, part.stop - part.start)
        large.append(pltpu.make_async_copy(field_hbm.at[place], field_ref.at[place], field_sems.at[i]))
    for copy in small[:1] + large[:2] + small[1:] + large[2:]:
        copy.start()

    def transform(i):
        large[i].wait()
        both = contract(table_ref[...], field_ref[parts[i]], (1, 1))
        spectra = both[:count] + both[count:]
        spectra_ref[:, parts[i]] = spectra
        narrow_ref[:, parts[i]] = spectra.astype(jnp.bfloat16)

    small[0].wait()
    transform(0)
    small[1].wait()
    small[2].wait()
    small[5].wait()
    build_operator(index, places, multiples, operator_ref)
    for i in range(1, len(parts) // 2):
        transform(i)
    small[3].wait()
    unpacked[...] = loaded[...].astype(jnp.float32)
    for block in range(NB):
        recorded_ref[:, block * 2 * BS : (block + 1) * 2 * BS] = unpacked[pl.ds(block, receivers, stride=NB), :]
    small[4].wait()
    shares, amount = max(halves) + 1, radius_ref.shape[1]
    for share in range(shares):
        rows_sent = radius[share * amount : (share + 1) * amount].astype(jnp.float32) + MARK * share
        for rank, half in enumerate(halves):
            if half == share:
                radius_ref[rank] = rows_sent.astype(jnp.bfloat16)
    for i in range(max(1, len(parts) // 2), len(parts)):
        transform(i)
    small[6].wait()


def forward(field, table, block_index, places, multiples, recorded, radius, distance, halves):
    rows, receivers = field.shape[0], radius.shape[1]
    count = table.shape[0] // 2
    arguments = (field, table, block_index, places, multiples, recorded, radius, distance)
    sent = (len(halves), radius.shape[0] // (max(halves) + 1), receivers)
    return pl.pallas_call(
        lambda *refs: forward_kernel(*refs, halves=halves),
        in_specs=[ANY] * 8,
        out_specs=[VMEM] * 8,
        out_shape=[
            jax.ShapeDtypeStruct((count, rows), jnp.bfloat16),
            pltpu.VMEM((count, rows), jnp.float32),
            pltpu.VMEM((rows, NT), jnp.bfloat16),
            pltpu.VMEM(table.shape, jnp.bfloat16),
            pltpu.VMEM((2 * SOURCES, WIDE), jnp.bfloat16),
            pltpu.VMEM((receivers, WIDE), jnp.float32),
            jax.ShapeDtypeStruct(sent, jnp.bfloat16),
            pltpu.VMEM(distance.shape, jnp.float32),
        ],
        scratch_shapes=[
            pltpu.SMEM((NB, BANDS), jnp.int32),
            pltpu.SMEM(places.shape, jnp.int32),
            pltpu.VMEM((NB, BANDS, BS, 2 * BS), jnp.bfloat16),
            pltpu.VMEM((receivers * NB, 2 * BS), jnp.bfloat16),
            pltpu.VMEM((receivers * NB, 2 * BS), jnp.float32),
            pltpu.VMEM(radius.shape, jnp.int32),
            pltpu.SemaphoreType.DMA((7,)),
            pltpu.SemaphoreType.DMA((len(chunks(rows)),)),
        ],
        compiler_params=params(16),
        name="forward_dft",
    )(*(pltpu.with_memory_space_constraint(a, pltpu.HBM) for a in arguments))


def gradient_of(returned_ref, table_ref, part):
    returned = returned_ref[:, part]
    return contract(jnp.concatenate([returned, returned], axis=0), table_ref[...], (0, 0))


def middle_kernel(start_ref, returned_ref, spectra_ref, table_ref, field_ref, narrow_ref, *, step):
    count, rows = spectra_ref.shape
    for i in range(rows // step):
        part = slice(i * step, (i + 1) * step)
        update = start_ref[part].astype(jnp.float32) + gradient_of(returned_ref, table_ref, part)
        clamped = clamp(update)
        field_ref[part] = update - clamped
        both = contract(table_ref[...], clamped.astype(jnp.bfloat16), (1, 1))
        linear = spectra_ref[:, part] + 0.5 * returned_ref[:, part].astype(jnp.float32)
        narrow_ref[:, part] = (linear - (both[:count] + both[count:])).astype(jnp.bfloat16)


def middle(start, returned, spectra, table):
    rows = start.shape[0]
    step = chunk_rows(rows, 768)
    return pl.pallas_call(
        lambda *refs: middle_kernel(*refs, step=step),
        in_specs=[VMEM] * 4,
        out_specs=[VMEM] * 2,
        out_shape=[pltpu.VMEM((rows, NT), jnp.float32), jax.ShapeDtypeStruct(spectra.shape, jnp.bfloat16)],
        compiler_params=params(16),
        name="update_and_forward",
    )(start, returned, spectra, table)


def final_kernel(field_ref, returned_ref, table_ref, out_hbm, buffer, sems):
    slots, step, _ = buffer.shape
    rows = field_ref.shape[0]
    copies = []
    for i in range(rows // step):
        if i >= slots:
            copies[i - slots].wait()
        part = slice(i * step, (i + 1) * step)
        update = field_ref[part] + gradient_of(returned_ref, table_ref, part)
        buffer[i % slots] = update - clamp(update)
        copies.append(
            pltpu.make_async_copy(buffer.at[i % slots], out_hbm.at[pl.ds(i * step, step)], sems.at[i % slots])
        )
        copies[i].start()
    for copy in copies[-slots:]:
        copy.wait()


def final(field, returned, table):
    rows = field.shape[0]
    step = chunk_rows(rows, 512)
    slots = min(4, rows // step)
    return pl.pallas_call(
        final_kernel,
        in_specs=[VMEM] * 3,
        out_specs=ANY,
        out_shape=pltpu.HBM((rows, NT), jnp.float32),
        scratch_shapes=[pltpu.VMEM((slots, step, NT), jnp.float32), pltpu.SemaphoreType.DMA((slots,))],
        compiler_params=params(16),
        name="last_update",
    )(field, returned, table)


def smooth(backward, radius, distance, returned_ref):
    sources, receivers = radius.shape
    rows = jnp.concatenate([backward[:sources], backward[sources:]], axis=1)
    narrow = rows.astype(jnp.bfloat16)
    radius = jnp.concatenate([radius, radius], axis=1)
    summed = rows
    for width in range(1, RADIUS + 1):
        band = jnp.where(distance <= width, 1.0, 0.0).astype(jnp.bfloat16)
        summed = jnp.where(radius >= width, contract(band, narrow, (1, 0)), summed)
    smoothed = (summed * (STEP / (2.0 * radius + 1.0))).astype(jnp.bfloat16)
    for part in range(2):
        own = smoothed[:, part * receivers : (part + 1) * receivers]
        if len(returned_ref.shape) == 4:
            returned_ref[:, part] = own.reshape(returned_ref.shape[0], *returned_ref.shape[2:])
        else:
            returned_ref[part * sources : (part + 1) * sources] = own


def adjoint(arrived_ref, operator_ref, recorded_ref):
    operator = operator_ref[...]
    if len(arrived_ref.shape) == 4:
        parts = [arrived_ref[:, part].reshape(SOURCES, arrived_ref.shape[3]) for part in range(2)]
        arrived = jnp.concatenate(parts, axis=0)
    else:
        arrived = arrived_ref[...]
    residual = recorded_ref[...] - contract(arrived, operator, (0, 0))
    return residual, contract(operator, residual.astype(jnp.bfloat16), (1, 1))


def first_owner_kernel(arrived_ref, operator_ref, recorded_ref, backward_ref):
    _, backward_ref[...] = adjoint(arrived_ref, operator_ref, recorded_ref)


def smooth_kernel(*refs):
    backward_ref, *halves, distance_ref, returned_ref, radius_ref = refs
    if len(halves) == 2:
        own, other = (half[...].astype(jnp.float32) for half in halves)
        both = jnp.stack([jnp.minimum(own, other), jnp.maximum(own, other) - MARK], axis=1)
        radius = both.reshape(radius_ref.shape)
    else:
        radius = halves[0][...].astype(jnp.float32)
    radius_ref[...] = radius
    smooth(backward_ref[...], radius, distance_ref[...], returned_ref)


def last_owner_kernel(
    arrived_ref, operator_ref, recorded_ref, radius_ref, distance_ref, returned_ref, residual_hbm, interleaved, sem
):
    residual, backward = adjoint(arrived_ref, operator_ref, recorded_ref)
    for block in range(NB):
        rows = pl.ds(block, residual.shape[0], stride=NB)
        interleaved[rows, :] = residual[:, block * 2 * BS : (block + 1) * 2 * BS]
    copy = pltpu.make_async_copy(interleaved, residual_hbm, sem)
    copy.start()
    smooth(backward, radius_ref[...], distance_ref[...], returned_ref)
    copy.wait()


def first_owner(arrived, operator, recorded):
    receivers = arrived.shape[1]
    return pl.pallas_call(
        first_owner_kernel,
        in_specs=[VMEM] * 3,
        out_specs=VMEM,
        out_shape=pltpu.VMEM((2 * SOURCES, receivers), jnp.float32),
        compiler_params=params(16),
        cost_estimate=pl.CostEstimate(
            flops=8 * receivers * SOURCES * WIDE, bytes_accessed=8 * receivers * WIDE, transcendentals=0
        ),
        name="owner_products",
    )(arrived, operator, recorded)


def smooth_sources(backward, radius, distance, shape):
    return pl.pallas_call(
        smooth_kernel,
        in_specs=[VMEM] * (2 + len(radius)),
        out_specs=[VMEM] * 2,
        out_shape=[
            jax.ShapeDtypeStruct(shape, jnp.bfloat16),
            pltpu.VMEM((SOURCES, backward.shape[1]), jnp.float32),
        ],
        compiler_params=params(16),
        name="smooth_sources",
    )(backward, *radius, distance)


def last_owner(arrived, operator, recorded, radius, distance, shape):
    receivers = recorded.shape[0]
    return pl.pallas_call(
        last_owner_kernel,
        in_specs=[VMEM] * 5,
        out_specs=[VMEM, ANY],
        out_shape=[
            jax.ShapeDtypeStruct(shape, jnp.bfloat16),
            pltpu.HBM((receivers * NB, 2 * BS), jnp.float32),
        ],
        scratch_shapes=[pltpu.VMEM((receivers * NB, 2 * BS), jnp.float32), pltpu.SemaphoreType.DMA(())],
        compiler_params=params(16),
        name="owner_step",
    )(arrived, operator, recorded, radius, distance)


def on_device(start_field, recorded, multiples, block_index, radius):
    devices = lax.axis_size("freq")
    local_src, receivers, _ = start_field.shape
    rows = local_src * receivers
    ranks = ranking(devices, local_src)
    places = row_places(ranks)
    whole_tiles = local_src % 16 == 0
    sent = (devices, 2, local_src, receivers) if whole_tiles else (2 * SOURCES, receivers)
    shares = 2 if devices % 2 == 0 and local_src % 2 == 0 else 1
    table = jnp.asarray(split_table(ranks))

    def exchange(pieces):
        return lax.all_to_all(pieces, "freq", split_axis=0, concat_axis=0, tiled=True, axis_index_groups=[ranks])

    def by_part(arrived):
        return arrived.reshape(devices, 2, local_src, receivers).swapaxes(0, 1).reshape(2 * SOURCES, receivers)

    def to_owners(narrow):
        arrived = exchange(narrow.reshape(devices, 2, local_src, receivers))
        return arrived if whole_tiles else by_part(arrived)

    def to_owners_with_radius(narrow, radius):
        rows = local_src // shares
        narrow = lax.optimization_barrier(narrow.reshape(devices, 2, local_src, receivers))
        pieces = [
            narrow.reshape(devices, 2 * shares, rows, receivers),
            radius.reshape(devices, 1, rows, receivers),
        ]
        arrived = exchange(jnp.concatenate(pieces, axis=1))
        halves = [arrived[:, 2 * shares]]
        if shares == 2:
            own, other = halves[0], lax.ppermute(halves[0], "freq", [(i, i ^ 1) for i in range(devices)])
            if whole_tiles:
                return by_part(arrived[:, : 2 * shares]), [own, other]
            halves = [jnp.minimum(own, other), jnp.maximum(own, other) - MARK]
        radius = jnp.stack(halves, axis=1).reshape(SOURCES, receivers)
        return by_part(arrived[:, : 2 * shares]), [radius]

    def to_traces(returned):
        if not whole_tiles:
            returned = returned.reshape(2, devices, local_src, receivers).swapaxes(0, 1)
        return exchange(returned).reshape(2 * devices, rows)

    narrow, spectra, start, table, operator, recorded, radius, distance = forward(
        start_field.reshape(rows, NT),
        table,
        block_index,
        jnp.asarray(places),
        multiples[0],
        recorded.reshape(-1, 2 * BS),
        radius,
        jnp.asarray(distances(ranks, local_src)),
        [rank % shares for rank in ranks],
    )
    arrived, radius = to_owners_with_radius(narrow, radius)
    returned, radius = smooth_sources(first_owner(arrived, operator, recorded), radius, distance, sent)
    field, narrow = middle(start, to_traces(returned), spectra, table)
    returned, residual = last_owner(to_owners(narrow), operator, recorded, radius, distance, sent)
    field = final(field, to_traces(returned), table)
    return field.reshape(local_src, receivers, NT), residual.reshape(1, receivers, NB, 2 * BS)


def solution(mesh):
    placed = (
        P(("grp", "freq"), None, None),
        P(("grp", "freq"), None, None, None),
        P(("grp", "freq"), None, None, None, None),
        P(),
        P(("grp", "freq"), None),
    )
    return jax.shard_map(
        on_device,
        mesh=mesh,
        in_specs=placed,
        out_specs=(P(("grp", "freq"), None, None), P(("grp", "freq"), None, None, None)),
        check_vma=False,
    )
```

```python
import math

import jax
import jax.numpy as jnp
import numpy as np
from jax import lax
from jax.experimental import pallas as pl
from jax.experimental.pallas import tpu as pltpu
from jax.sharding import PartitionSpec as P

NB = 4
BS = 64
BANDS = 3
NT = 512
RADIUS = 4
STEP = 0.5
MARK = 8
RANKS = (11, 13, 15, 1, 3, 6, 5, 9, 2, 7, 4, 14, 8, 12, 10, 0)
SHRINKAGE = 0.05
SOURCES = NB * BS
WIDE = NB * 2 * BS
MIB = 1 << 20
VMEM = pl.BlockSpec(memory_space=pltpu.VMEM)
ANY = pl.BlockSpec(memory_space=pl.ANY)


def ranking(devices, local_src):
    fits = devices == len(RANKS) and local_src % 16 == 0 and BS % local_src == 0
    return list(RANKS) if fits else list(range(devices))


def split_table(ranks):
    phases = np.arange(NT)[:, None] * (np.array(ranks) + 1)[None, :] % NT
    angles = phases * (2.0 * math.pi / NT)
    table = np.stack([np.cos(angles), -np.sin(angles)], axis=-1).reshape(NT, 2 * len(ranks)) / math.sqrt(NT)
    table = table.T.astype(np.float32)
    upper = table.astype(jnp.bfloat16)
    lower = (table - upper.astype(np.float32)).astype(jnp.bfloat16)
    return np.concatenate([upper, lower], axis=0)


def row_places(ranks):
    return np.arange(NB, dtype=np.int32) if ranks == sorted(ranks) else np.argsort(ranks).astype(np.int32)


def distances(ranks, local_src):
    sources = (np.array(ranks)[:, None] * local_src + np.arange(local_src)).reshape(-1)
    return np.abs(sources[:, None] - sources[None, :]).astype(np.float32)


def contract(a, b, dims):
    return lax.dot_general(a, b, ((dims[:1], dims[1:]), ((), ())), preferred_element_type=jnp.float32)


def clamp(u):
    return jnp.clip(u, -SHRINKAGE, SHRINKAGE)


def params(limit):
    return pltpu.CompilerParams(vmem_limit_bytes=limit * MIB)


def chunk_rows(rows, most):
    return max(size for size in range(128, most + 1, 128) if rows % size == 0)


def chunks(rows):
    unit = rows // 128 // 6 * 128
    bounds = [0, unit, 2 * unit, 4 * unit, rows] if unit else [0, rows]
    return [slice(low, high) for low, high in zip(bounds[:-1], bounds[1:])]


def build_operator(index_ref, places_ref, multiples_ref, operator_ref):
    operator_ref[...] = jnp.zeros_like(operator_ref)
    runs = places_ref.shape[0] // NB
    length = BS // runs
    for block in range(NB):
        columns = slice(block * 2 * BS, (block + 1) * 2 * BS)
        for band in range(BANDS):
            pair = multiples_ref[block, band]
            turned = jnp.concatenate([-pair[:, BS:], pair[:, :BS]], axis=1)
            for run in range(runs):
                first = pl.multiple_of(places_ref[index_ref[block, band] * runs + run] * length, length)
                part = slice(run * length, (run + 1) * length)
                operator_ref[pl.ds(first, length), columns] = pair[part]
                operator_ref[pl.ds(SOURCES + first, length), columns] = turned[part]


def forward_kernel(
    field_hbm, table_hbm, index_hbm, places_hbm, multiples_hbm, recorded_hbm, radius_hbm, distance_hbm,
    narrow_ref, spectra_ref, field_ref, table_ref, operator_ref, recorded_ref, radius_ref, distance_ref,
    index, places, multiples, loaded, radius, sems, field_sems, *, halves,
):
    count, rows = spectra_ref.shape
    parts = chunks(rows)
    small = [
        pltpu.make_async_copy(table_hbm, table_ref, sems.at[0]),
        pltpu.make_async_copy(index_hbm, index, sems.at[1]),
        pltpu.make_async_copy(multiples_hbm, multiples, sems.at[2]),
        pltpu.make_async_copy(recorded_hbm, loaded, sems.at[3]),
        pltpu.make_async_copy(radius_hbm, radius, sems.at[4]),
        pltpu.make_async_copy(places_hbm, places, sems.at[5]),
        pltpu.make_async_copy(distance_hbm, distance_ref, sems.at[6]),
    ]
    large = []
    for i, part in enumerate(parts):
        place = pl.ds(part.start, part.stop - part.start)
        large.append(pltpu.make_async_copy(field_hbm.at[place], field_ref.at[place], field_sems.at[i]))
    for copy in small[:1] + large[:2] + small[1:] + large[2:]:
        copy.start()

    def transform(i):
        large[i].wait()
        both = contract(table_ref[...], field_ref[parts[i]], (1, 1))
        spectra = both[:count] + both[count:]
        spectra_ref[:, parts[i]] = spectra
        narrow_ref[:, parts[i]] = spectra.astype(jnp.bfloat16)

    small[0].wait()
    transform(0)
    small[1].wait()
    small[2].wait()
    small[5].wait()
    build_operator(index, places, multiples, operator_ref)
    for i in range(1, len(parts) // 2):
        transform(i)
    small[3].wait()
    recorded_ref[...] = loaded[...].astype(jnp.float32)
    small[4].wait()
    shares, amount = max(halves) + 1, radius_ref.shape[1]
    for share in range(shares):
        rows_sent = radius[share * amount : (share + 1) * amount].astype(jnp.float32) + MARK * share
        for rank, half in enumerate(halves):
            if half == share:
                radius_ref[rank] = rows_sent.astype(jnp.bfloat16)
    for i in range(max(1, len(parts) // 2), len(parts)):
        transform(i)
    small[6].wait()


def forward(field, table, block_index, places, multiples, recorded, radius, distance, halves):
    rows, receivers = field.shape[0], radius.shape[1]
    count = table.shape[0] // 2
    arguments = (field, table, block_index, places, multiples, recorded, radius, distance)
    sent = (len(halves), radius.shape[0] // (max(halves) + 1), receivers)
    return pl.pallas_call(
        lambda *refs: forward_kernel(*refs, halves=halves),
        in_specs=[ANY] * 8,
        out_specs=[VMEM] * 8,
        out_shape=[
            jax.ShapeDtypeStruct((count, rows), jnp.bfloat16),
            pltpu.VMEM((count, rows), jnp.float32),
            pltpu.VMEM((rows, NT), jnp.bfloat16),
            pltpu.VMEM(table.shape, jnp.bfloat16),
            pltpu.VMEM((2 * SOURCES, WIDE), jnp.bfloat16),
            pltpu.VMEM((receivers * NB, 2 * BS), jnp.float32),
            jax.ShapeDtypeStruct(sent, jnp.bfloat16),
            pltpu.VMEM(distance.shape, jnp.float32),
        ],
        scratch_shapes=[
            pltpu.SMEM((NB, BANDS), jnp.int32),
            pltpu.SMEM(places.shape, jnp.int32),
            pltpu.VMEM((NB, BANDS, BS, 2 * BS), jnp.bfloat16),
            pltpu.VMEM((receivers * NB, 2 * BS), jnp.bfloat16),
            pltpu.VMEM(radius.shape, jnp.int32),
            pltpu.SemaphoreType.DMA((7,)),
            pltpu.SemaphoreType.DMA((len(chunks(rows)),)),
        ],
        compiler_params=params(16),
        name="forward_dft",
    )(*(pltpu.with_memory_space_constraint(a, pltpu.HBM) for a in arguments))


def gradient_of(returned_ref, table_ref, part):
    returned = returned_ref[:, part]
    return contract(jnp.concatenate([returned, returned], axis=0), table_ref[...], (0, 0))


def middle_kernel(start_ref, returned_ref, spectra_ref, table_ref, field_ref, narrow_ref, *, step):
    count, rows = spectra_ref.shape
    for i in range(rows // step):
        part = slice(i * step, (i + 1) * step)
        update = start_ref[part].astype(jnp.float32) + gradient_of(returned_ref, table_ref, part)
        clamped = clamp(update)
        field_ref[part] = update - clamped
        both = contract(table_ref[...], clamped.astype(jnp.bfloat16), (1, 1))
        linear = spectra_ref[:, part] + 0.5 * returned_ref[:, part].astype(jnp.float32)
        narrow_ref[:, part] = (linear - (both[:count] + both[count:])).astype(jnp.bfloat16)


def middle(start, returned, spectra, table):
    rows = start.shape[0]
    step = chunk_rows(rows, 768)
    return pl.pallas_call(
        lambda *refs: middle_kernel(*refs, step=step),
        in_specs=[VMEM] * 4,
        out_specs=[VMEM] * 2,
        out_shape=[pltpu.VMEM((rows, NT), jnp.float32), jax.ShapeDtypeStruct(spectra.shape, jnp.bfloat16)],
        compiler_params=params(16),
        name="update_and_forward",
    )(start, returned, spectra, table)


def final_kernel(field_ref, returned_ref, table_ref, out_hbm, buffer, sems):
    slots, step, _ = buffer.shape
    rows = field_ref.shape[0]
    copies = []
    for i in range(rows // step):
        if i >= slots:
            copies[i - slots].wait()
        part = slice(i * step, (i + 1) * step)
        update = field_ref[part] + gradient_of(returned_ref, table_ref, part)
        buffer[i % slots] = update - clamp(update)
        copies.append(
            pltpu.make_async_copy(buffer.at[i % slots], out_hbm.at[pl.ds(i * step, step)], sems.at[i % slots])
        )
        copies[i].start()
    for copy in copies[-slots:]:
        copy.wait()


def final(field, returned, table):
    rows = field.shape[0]
    step = chunk_rows(rows, 512)
    slots = min(4, rows // step)
    return pl.pallas_call(
        final_kernel,
        in_specs=[VMEM] * 3,
        out_specs=ANY,
        out_shape=pltpu.HBM((rows, NT), jnp.float32),
        scratch_shapes=[pltpu.VMEM((slots, step, NT), jnp.float32), pltpu.SemaphoreType.DMA((slots,))],
        compiler_params=params(16),
        name="last_update",
    )(field, returned, table)


def smooth(backward, radius, distance, returned_ref):
    sources, receivers = radius.shape
    rows = jnp.concatenate([backward[:sources], backward[sources:]], axis=1)
    narrow = rows.astype(jnp.bfloat16)
    radius = jnp.concatenate([radius, radius], axis=1)
    summed = rows
    for width in range(1, RADIUS + 1):
        band = jnp.where(distance <= width, 1.0, 0.0).astype(jnp.bfloat16)
        summed = jnp.where(radius >= width, contract(band, narrow, (1, 0)), summed)
    smoothed = (summed * (STEP / (2.0 * radius + 1.0))).astype(jnp.bfloat16)
    for part in range(2):
        own = smoothed[:, part * receivers : (part + 1) * receivers]
        if len(returned_ref.shape) == 4:
            returned_ref[:, part] = own.reshape(returned_ref.shape[0], *returned_ref.shape[2:])
        else:
            returned_ref[part * sources : (part + 1) * sources] = own


def adjoint(arrived_ref, operator_ref, recorded_ref):
    operator = operator_ref[...]
    if len(arrived_ref.shape) == 4:
        parts = [arrived_ref[:, part].reshape(SOURCES, arrived_ref.shape[3]) for part in range(2)]
        arrived = jnp.concatenate(parts, axis=0)
    else:
        arrived = arrived_ref[...]
    receivers = recorded_ref.shape[0] // NB
    blocks = [recorded_ref[pl.ds(block, receivers, stride=NB), :] for block in range(NB)]
    residual = jnp.concatenate(blocks, axis=1) - contract(arrived, operator, (0, 0))
    return residual, contract(operator, residual.astype(jnp.bfloat16), (1, 1))


def first_owner_kernel(arrived_ref, operator_ref, recorded_ref, backward_ref):
    _, backward_ref[...] = adjoint(arrived_ref, operator_ref, recorded_ref)


def smooth_kernel(*refs):
    backward_ref, *halves, distance_ref, returned_ref, radius_ref = refs
    if len(halves) == 2:
        own, other = (half[...].astype(jnp.float32) for half in halves)
        both = jnp.stack([jnp.minimum(own, other), jnp.maximum(own, other) - MARK], axis=1)
        radius = both.reshape(radius_ref.shape)
    else:
        radius = halves[0][...].astype(jnp.float32)
    radius_ref[...] = radius
    smooth(backward_ref[...], radius, distance_ref[...], returned_ref)


def last_owner_kernel(
    arrived_ref, operator_ref, recorded_ref, radius_ref, distance_ref, returned_ref, residual_hbm, interleaved, sem
):
    residual, backward = adjoint(arrived_ref, operator_ref, recorded_ref)
    for block in range(NB):
        rows = pl.ds(block, residual.shape[0], stride=NB)
        interleaved[rows, :] = residual[:, block * 2 * BS : (block + 1) * 2 * BS]
    copy = pltpu.make_async_copy(interleaved, residual_hbm, sem)
    copy.start()
    smooth(backward, radius_ref[...], distance_ref[...], returned_ref)
    copy.wait()


def first_owner(arrived, operator, recorded):
    receivers = recorded.shape[0] // NB
    return pl.pallas_call(
        first_owner_kernel,
        in_specs=[VMEM] * 3,
        out_specs=VMEM,
        out_shape=pltpu.VMEM((2 * SOURCES, receivers), jnp.float32),
        compiler_params=params(16),
        cost_estimate=pl.CostEstimate(
            flops=8 * receivers * SOURCES * WIDE, bytes_accessed=8 * receivers * WIDE, transcendentals=0
        ),
        name="owner_products",
    )(arrived, operator, recorded)


def smooth_sources(backward, radius, distance, shape):
    return pl.pallas_call(
        smooth_kernel,
        in_specs=[VMEM] * (2 + len(radius)),
        out_specs=[VMEM] * 2,
        out_shape=[
            jax.ShapeDtypeStruct(shape, jnp.bfloat16),
            pltpu.VMEM((SOURCES, backward.shape[1]), jnp.float32),
        ],
        compiler_params=params(16),
        name="smooth_sources",
    )(backward, *radius, distance)


def last_owner(arrived, operator, recorded, radius, distance, shape):
    receivers = recorded.shape[0] // NB
    return pl.pallas_call(
        last_owner_kernel,
        in_specs=[VMEM] * 5,
        out_specs=[VMEM, ANY],
        out_shape=[
            jax.ShapeDtypeStruct(shape, jnp.bfloat16),
            pltpu.HBM((receivers * NB, 2 * BS), jnp.float32),
        ],
        scratch_shapes=[pltpu.VMEM((receivers * NB, 2 * BS), jnp.float32), pltpu.SemaphoreType.DMA(())],
        compiler_params=params(16),
        name="owner_step",
    )(arrived, operator, recorded, radius, distance)


def on_device(start_field, recorded, multiples, block_index, radius):
    devices = lax.axis_size("freq")
    local_src, receivers, _ = start_field.shape
    rows = local_src * receivers
    ranks = ranking(devices, local_src)
    places = row_places(ranks)
    whole_tiles = local_src % 16 == 0
    sent = (devices, 2, local_src, receivers) if whole_tiles else (2 * SOURCES, receivers)
    shares = 2 if devices % 2 == 0 and local_src % 2 == 0 else 1
    table = jnp.asarray(split_table(ranks))

    def exchange(pieces):
        return lax.all_to_all(pieces, "freq", split_axis=0, concat_axis=0, tiled=True, axis_index_groups=[ranks])

    def by_part(arrived):
        return arrived.reshape(devices, 2, local_src, receivers).swapaxes(0, 1).reshape(2 * SOURCES, receivers)

    def to_owners(narrow):
        arrived = exchange(narrow.reshape(devices, 2, local_src, receivers))
        return arrived if whole_tiles else by_part(arrived)

    def to_owners_with_radius(narrow, radius):
        rows = local_src // shares
        narrow = lax.optimization_barrier(narrow.reshape(devices, 2, local_src, receivers))
        pieces = [
            narrow.reshape(devices, 2 * shares, rows, receivers),
            radius.reshape(devices, 1, rows, receivers),
        ]
        arrived = exchange(jnp.concatenate(pieces, axis=1))
        halves = [arrived[:, 2 * shares]]
        if shares == 2:
            own, other = halves[0], lax.ppermute(halves[0], "freq", [(i, i ^ 1) for i in range(devices)])
            if whole_tiles:
                return by_part(arrived[:, : 2 * shares]), [own, other]
            halves = [jnp.minimum(own, other), jnp.maximum(own, other) - MARK]
        radius = jnp.stack(halves, axis=1).reshape(SOURCES, receivers)
        return by_part(arrived[:, : 2 * shares]), [radius]

    def to_traces(returned):
        if not whole_tiles:
            returned = returned.reshape(2, devices, local_src, receivers).swapaxes(0, 1)
        return exchange(returned).reshape(2 * devices, rows)

    narrow, spectra, start, table, operator, recorded, radius, distance = forward(
        start_field.reshape(rows, NT),
        table,
        block_index,
        jnp.asarray(places),
        multiples[0],
        recorded.reshape(-1, 2 * BS),
        radius,
        jnp.asarray(distances(ranks, local_src)),
        [rank % shares for rank in ranks],
    )
    arrived, radius = to_owners_with_radius(narrow, radius)
    returned, radius = smooth_sources(first_owner(arrived, operator, recorded), radius, distance, sent)
    field, narrow = middle(start, to_traces(returned), spectra, table)
    returned, residual = last_owner(to_owners(narrow), operator, recorded, radius, distance, sent)
    field = final(field, to_traces(returned), table)
    return field.reshape(local_src, receivers, NT), residual.reshape(1, receivers, NB, 2 * BS)


def solution(mesh):
    placed = (
        P(("grp", "freq"), None, None),
        P(("grp", "freq"), None, None, None),
        P(("grp", "freq"), None, None, None, None),
        P(),
        P(("grp", "freq"), None),
    )
    return jax.shard_map(
        on_device,
        mesh=mesh,
        in_specs=placed,
        out_specs=(P(("grp", "freq"), None, None), P(("grp", "freq"), None, None, None)),
        check_vma=False,
    )
```

```python
import math

import jax
import jax.numpy as jnp
import numpy as np
from jax import lax
from jax.experimental import pallas as pl
from jax.experimental.pallas import tpu as pltpu
from jax.sharding import PartitionSpec as P

NB = 4
BS = 64
BANDS = 3
NT = 512
RADIUS = 4
STEP = 0.5
MARK = 8
RANKS = (11, 13, 15, 1, 3, 6, 5, 9, 2, 7, 4, 14, 8, 12, 10, 0)
SHRINKAGE = 0.05
SOURCES = NB * BS
WIDE = NB * 2 * BS
MIB = 1 << 20
VMEM = pl.BlockSpec(memory_space=pltpu.VMEM)
ANY = pl.BlockSpec(memory_space=pl.ANY)


def ranking(devices, local_src):
    fits = devices == len(RANKS) and local_src % 16 == 0 and BS % local_src == 0
    return list(RANKS) if fits else list(range(devices))


def split_table(ranks):
    phases = np.arange(NT)[:, None] * (np.array(ranks) + 1)[None, :] % NT
    angles = phases * (2.0 * math.pi / NT)
    table = np.stack([np.cos(angles), -np.sin(angles)], axis=-1).reshape(NT, 2 * len(ranks)) / math.sqrt(NT)
    table = table.T.astype(np.float32)
    upper = table.astype(jnp.bfloat16)
    lower = (table - upper.astype(np.float32)).astype(jnp.bfloat16)
    return np.concatenate([upper, lower], axis=0)


def row_places(ranks):
    return np.arange(NB, dtype=np.int32) if ranks == sorted(ranks) else np.argsort(ranks).astype(np.int32)


def distances(ranks, local_src):
    sources = (np.array(ranks)[:, None] * local_src + np.arange(local_src)).reshape(-1)
    return np.abs(sources[:, None] - sources[None, :]).astype(np.float32)


def contract(a, b, dims):
    return lax.dot_general(a, b, ((dims[:1], dims[1:]), ((), ())), preferred_element_type=jnp.float32)


def clamp(u):
    return jnp.clip(u, -SHRINKAGE, SHRINKAGE)


def params(limit):
    return pltpu.CompilerParams(vmem_limit_bytes=limit * MIB)


def chunk_rows(rows, most):
    return max(size for size in range(128, most + 1, 128) if rows % size == 0)


def chunks(rows):
    unit = rows // 128 // 6 * 128
    bounds = [0, unit, 2 * unit, 4 * unit, 5 * unit, rows] if unit else [0, rows]
    return [slice(low, high) for low, high in zip(bounds[:-1], bounds[1:])]


def build_operator(index_ref, places_ref, multiples_ref, operator_ref):
    operator_ref[...] = jnp.zeros_like(operator_ref)
    runs = places_ref.shape[0] // NB
    length = BS // runs
    for block in range(NB):
        columns = slice(block * 2 * BS, (block + 1) * 2 * BS)
        for band in range(BANDS):
            pair = multiples_ref[block, band]
            turned = jnp.concatenate([-pair[:, BS:], pair[:, :BS]], axis=1)
            for run in range(runs):
                first = pl.multiple_of(places_ref[index_ref[block, band] * runs + run] * length, length)
                part = slice(run * length, (run + 1) * length)
                operator_ref[pl.ds(first, length), columns] = pair[part]
                operator_ref[pl.ds(SOURCES + first, length), columns] = turned[part]


def forward_kernel(
    field_hbm, table_hbm, index_hbm, places_hbm, multiples_hbm, recorded_hbm, radius_hbm, distance_hbm,
    narrow_ref, spectra_ref, field_ref, table_ref, operator_ref, recorded_ref, radius_ref, distance_ref,
    index, places, multiples, loaded, radius, sems, field_sems, *, halves,
):
    count, rows = spectra_ref.shape
    parts = chunks(rows)
    small = [
        pltpu.make_async_copy(table_hbm, table_ref, sems.at[0]),
        pltpu.make_async_copy(index_hbm, index, sems.at[1]),
        pltpu.make_async_copy(multiples_hbm, multiples, sems.at[2]),
        pltpu.make_async_copy(recorded_hbm, loaded, sems.at[3]),
        pltpu.make_async_copy(radius_hbm, radius, sems.at[4]),
        pltpu.make_async_copy(places_hbm, places, sems.at[5]),
        pltpu.make_async_copy(distance_hbm, distance_ref, sems.at[6]),
    ]
    large = []
    for i, part in enumerate(parts):
        place = pl.ds(part.start, part.stop - part.start)
        large.append(pltpu.make_async_copy(field_hbm.at[place], field_ref.at[place], field_sems.at[i]))
    for copy in small[:1] + large[:2] + small[1:] + large[2:]:
        copy.start()

    def transform(i):
        large[i].wait()
        both = contract(table_ref[...], field_ref[parts[i]], (1, 1))
        spectra = both[:count] + both[count:]
        spectra_ref[:, parts[i]] = spectra
        narrow_ref[:, parts[i]] = spectra.astype(jnp.bfloat16)

    small[0].wait()
    transform(0)
    small[1].wait()
    small[2].wait()
    small[5].wait()
    build_operator(index, places, multiples, operator_ref)
    for i in range(1, len(parts) // 2):
        transform(i)
    small[3].wait()
    recorded_ref[...] = loaded[...].astype(jnp.float32)
    small[4].wait()
    shares, amount = max(halves) + 1, radius_ref.shape[1]
    for share in range(shares):
        rows_sent = radius[share * amount : (share + 1) * amount].astype(jnp.float32) + MARK * share
        for rank, half in enumerate(halves):
            if half == share:
                radius_ref[rank] = rows_sent.astype(jnp.bfloat16)
    for i in range(max(1, len(parts) // 2), len(parts)):
        transform(i)
    small[6].wait()


def forward(field, table, block_index, places, multiples, recorded, radius, distance, halves):
    rows, receivers = field.shape[0], radius.shape[1]
    count = table.shape[0] // 2
    arguments = (field, table, block_index, places, multiples, recorded, radius, distance)
    sent = (len(halves), radius.shape[0] // (max(halves) + 1), receivers)
    return pl.pallas_call(
        lambda *refs: forward_kernel(*refs, halves=halves),
        in_specs=[ANY] * 8,
        out_specs=[VMEM] * 8,
        out_shape=[
            jax.ShapeDtypeStruct((count, rows), jnp.bfloat16),
            pltpu.VMEM((count, rows), jnp.float32),
            pltpu.VMEM((rows, NT), jnp.bfloat16),
            pltpu.VMEM(table.shape, jnp.bfloat16),
            pltpu.VMEM((2 * SOURCES, WIDE), jnp.bfloat16),
            pltpu.VMEM((receivers * NB, 2 * BS), jnp.float32),
            jax.ShapeDtypeStruct(sent, jnp.bfloat16),
            pltpu.VMEM(distance.shape, jnp.float32),
        ],
        scratch_shapes=[
            pltpu.SMEM((NB, BANDS), jnp.int32),
            pltpu.SMEM(places.shape, jnp.int32),
            pltpu.VMEM((NB, BANDS, BS, 2 * BS), jnp.bfloat16),
            pltpu.VMEM((receivers * NB, 2 * BS), jnp.bfloat16),
            pltpu.VMEM(radius.shape, jnp.int32),
            pltpu.SemaphoreType.DMA((7,)),
            pltpu.SemaphoreType.DMA((len(chunks(rows)),)),
        ],
        compiler_params=params(16),
        name="forward_dft",
    )(*(pltpu.with_memory_space_constraint(a, pltpu.HBM) for a in arguments))


def gradient_of(returned_ref, table_ref, part):
    returned = returned_ref[:, part]
    return contract(jnp.concatenate([returned, returned], axis=0), table_ref[...], (0, 0))


def middle_kernel(start_ref, returned_ref, spectra_ref, table_ref, field_ref, narrow_ref, *, step):
    count, rows = spectra_ref.shape
    for i in range(rows // step):
        part = slice(i * step, (i + 1) * step)
        update = start_ref[part].astype(jnp.float32) + gradient_of(returned_ref, table_ref, part)
        clamped = clamp(update)
        field_ref[part] = update - clamped
        both = contract(table_ref[...], clamped.astype(jnp.bfloat16), (1, 1))
        linear = spectra_ref[:, part] + 0.5 * returned_ref[:, part].astype(jnp.float32)
        narrow_ref[:, part] = (linear - (both[:count] + both[count:])).astype(jnp.bfloat16)


def middle(start, returned, spectra, table):
    rows = start.shape[0]
    step = chunk_rows(rows, 768)
    return pl.pallas_call(
        lambda *refs: middle_kernel(*refs, step=step),
        in_specs=[VMEM] * 4,
        out_specs=[VMEM] * 2,
        out_shape=[pltpu.VMEM((rows, NT), jnp.float32), jax.ShapeDtypeStruct(spectra.shape, jnp.bfloat16)],
        compiler_params=params(16),
        name="update_and_forward",
    )(start, returned, spectra, table)


def final_kernel(field_ref, returned_ref, table_ref, out_hbm, buffer, sems):
    slots, step, _ = buffer.shape
    rows = field_ref.shape[0]
    copies = []
    for i in range(rows // step):
        if i >= slots:
            copies[i - slots].wait()
        part = slice(i * step, (i + 1) * step)
        update = field_ref[part] + gradient_of(returned_ref, table_ref, part)
        buffer[i % slots] = update - clamp(update)
        copies.append(
            pltpu.make_async_copy(buffer.at[i % slots], out_hbm.at[pl.ds(i * step, step)], sems.at[i % slots])
        )
        copies[i].start()
    for copy in copies[-slots:]:
        copy.wait()


def final(field, returned, table):
    rows = field.shape[0]
    step = chunk_rows(rows, 512)
    slots = min(4, rows // step)
    return pl.pallas_call(
        final_kernel,
        in_specs=[VMEM] * 3,
        out_specs=ANY,
        out_shape=pltpu.HBM((rows, NT), jnp.float32),
        scratch_shapes=[pltpu.VMEM((slots, step, NT), jnp.float32), pltpu.SemaphoreType.DMA((slots,))],
        compiler_params=params(16),
        name="last_update",
    )(field, returned, table)


def smooth(backward, radius, distance, returned_ref):
    sources, receivers = radius.shape
    rows = jnp.concatenate([backward[:sources], backward[sources:]], axis=1)
    narrow = rows.astype(jnp.bfloat16)
    radius = jnp.concatenate([radius, radius], axis=1)
    summed = rows
    for width in range(1, RADIUS + 1):
        band = jnp.where(distance <= width, 1.0, 0.0).astype(jnp.bfloat16)
        summed = jnp.where(radius >= width, contract(band, narrow, (1, 0)), summed)
    smoothed = (summed * (STEP / (2.0 * radius + 1.0))).astype(jnp.bfloat16)
    for part in range(2):
        own = smoothed[:, part * receivers : (part + 1) * receivers]
        if len(returned_ref.shape) == 4:
            returned_ref[:, part] = own.reshape(returned_ref.shape[0], *returned_ref.shape[2:])
        else:
            returned_ref[part * sources : (part + 1) * sources] = own


def adjoint(arrived_ref, operator_ref, recorded_ref):
    operator = operator_ref[...]
    if len(arrived_ref.shape) == 4:
        parts = [arrived_ref[:, part].reshape(SOURCES, arrived_ref.shape[3]) for part in range(2)]
        arrived = jnp.concatenate(parts, axis=0)
    else:
        arrived = arrived_ref[...]
    receivers = recorded_ref.shape[0] // NB
    blocks = [recorded_ref[pl.ds(block, receivers, stride=NB), :] for block in range(NB)]
    residual = jnp.concatenate(blocks, axis=1) - contract(arrived, operator, (0, 0))
    return residual, contract(operator, residual.astype(jnp.bfloat16), (1, 1))


def first_owner_kernel(arrived_ref, operator_ref, recorded_ref, backward_ref):
    _, backward_ref[...] = adjoint(arrived_ref, operator_ref, recorded_ref)


def smooth_kernel(*refs):
    backward_ref, *halves, distance_ref, returned_ref, radius_ref = refs
    if len(halves) == 2:
        own, other = (half[...].astype(jnp.float32) for half in halves)
        both = jnp.stack([jnp.minimum(own, other), jnp.maximum(own, other) - MARK], axis=1)
        radius = both.reshape(radius_ref.shape)
    else:
        radius = halves[0][...].astype(jnp.float32)
    radius_ref[...] = radius
    smooth(backward_ref[...], radius, distance_ref[...], returned_ref)


def last_owner_kernel(
    arrived_ref, operator_ref, recorded_ref, radius_ref, distance_ref, returned_ref, residual_hbm, interleaved, sem
):
    residual, backward = adjoint(arrived_ref, operator_ref, recorded_ref)
    for block in range(NB):
        rows = pl.ds(block, residual.shape[0], stride=NB)
        interleaved[rows, :] = residual[:, block * 2 * BS : (block + 1) * 2 * BS]
    copy = pltpu.make_async_copy(interleaved, residual_hbm, sem)
    copy.start()
    smooth(backward, radius_ref[...], distance_ref[...], returned_ref)
    copy.wait()


def first_owner(arrived, operator, recorded):
    receivers = recorded.shape[0] // NB
    return pl.pallas_call(
        first_owner_kernel,
        in_specs=[VMEM] * 3,
        out_specs=VMEM,
        out_shape=pltpu.VMEM((2 * SOURCES, receivers), jnp.float32),
        compiler_params=params(16),
        cost_estimate=pl.CostEstimate(
            flops=8 * receivers * SOURCES * WIDE, bytes_accessed=8 * receivers * WIDE, transcendentals=0
        ),
        name="owner_products",
    )(arrived, operator, recorded)


def smooth_sources(backward, radius, distance, shape):
    return pl.pallas_call(
        smooth_kernel,
        in_specs=[VMEM] * (2 + len(radius)),
        out_specs=[VMEM] * 2,
        out_shape=[
            jax.ShapeDtypeStruct(shape, jnp.bfloat16),
            pltpu.VMEM((SOURCES, backward.shape[1]), jnp.float32),
        ],
        compiler_params=params(16),
        name="smooth_sources",
    )(backward, *radius, distance)


def last_owner(arrived, operator, recorded, radius, distance, shape):
    receivers = recorded.shape[0] // NB
    return pl.pallas_call(
        last_owner_kernel,
        in_specs=[VMEM] * 5,
        out_specs=[VMEM, ANY],
        out_shape=[
            jax.ShapeDtypeStruct(shape, jnp.bfloat16),
            pltpu.HBM((receivers * NB, 2 * BS), jnp.float32),
        ],
        scratch_shapes=[pltpu.VMEM((receivers * NB, 2 * BS), jnp.float32), pltpu.SemaphoreType.DMA(())],
        compiler_params=params(16),
        name="owner_step",
    )(arrived, operator, recorded, radius, distance)


def on_device(start_field, recorded, multiples, block_index, radius):
    devices = lax.axis_size("freq")
    local_src, receivers, _ = start_field.shape
    rows = local_src * receivers
    ranks = ranking(devices, local_src)
    places = row_places(ranks)
    whole_tiles = local_src % 16 == 0
    sent = (devices, 2, local_src, receivers) if whole_tiles else (2 * SOURCES, receivers)
    shares = 2 if devices % 2 == 0 and local_src % 2 == 0 else 1
    table = jnp.asarray(split_table(ranks))

    def exchange(pieces):
        return lax.all_to_all(pieces, "freq", split_axis=0, concat_axis=0, tiled=True, axis_index_groups=[ranks])

    def by_part(arrived):
        return arrived.reshape(devices, 2, local_src, receivers).swapaxes(0, 1).reshape(2 * SOURCES, receivers)

    def to_owners(narrow):
        arrived = exchange(narrow.reshape(devices, 2, local_src, receivers))
        return arrived if whole_tiles else by_part(arrived)

    def to_owners_with_radius(narrow, radius):
        rows = local_src // shares
        narrow = lax.optimization_barrier(narrow.reshape(devices, 2, local_src, receivers))
        pieces = [
            narrow.reshape(devices, 2 * shares, rows, receivers),
            radius.reshape(devices, 1, rows, receivers),
        ]
        arrived = exchange(jnp.concatenate(pieces, axis=1))
        halves = [arrived[:, 2 * shares]]
        if shares == 2:
            own, other = halves[0], lax.ppermute(halves[0], "freq", [(i, i ^ 1) for i in range(devices)])
            if whole_tiles:
                return by_part(arrived[:, : 2 * shares]), [own, other]
            halves = [jnp.minimum(own, other), jnp.maximum(own, other) - MARK]
        radius = jnp.stack(halves, axis=1).reshape(SOURCES, receivers)
        return by_part(arrived[:, : 2 * shares]), [radius]

    def to_traces(returned):
        if not whole_tiles:
            returned = returned.reshape(2, devices, local_src, receivers).swapaxes(0, 1)
        return exchange(returned).reshape(2 * devices, rows)

    narrow, spectra, start, table, operator, recorded, radius, distance = forward(
        start_field.reshape(rows, NT),
        table,
        block_index,
        jnp.asarray(places),
        multiples[0],
        recorded.reshape(-1, 2 * BS),
        radius,
        jnp.asarray(distances(ranks, local_src)),
        [rank % shares for rank in ranks],
    )
    arrived, radius = to_owners_with_radius(narrow, radius)
    returned, radius = smooth_sources(first_owner(arrived, operator, recorded), radius, distance, sent)
    field, narrow = middle(start, to_traces(returned), spectra, table)
    returned, residual = last_owner(to_owners(narrow), operator, recorded, radius, distance, sent)
    field = final(field, to_traces(returned), table)
    return field.reshape(local_src, receivers, NT), residual.reshape(1, receivers, NB, 2 * BS)


def solution(mesh):
    placed = (
        P(("grp", "freq"), None, None),
        P(("grp", "freq"), None, None, None),
        P(("grp", "freq"), None, None, None, None),
        P(),
        P(("grp", "freq"), None),
    )
    return jax.shard_map(
        on_device,
        mesh=mesh,
        in_specs=placed,
        out_specs=(P(("grp", "freq"), None, None), P(("grp", "freq"), None, None, None)),
        check_vma=False,
    )
```

```python
import math

import jax
import jax.numpy as jnp
import numpy as np
from jax import lax
from jax.experimental import pallas as pl
from jax.experimental.pallas import tpu as pltpu
from jax.sharding import PartitionSpec as P

NB = 4
BS = 64
BANDS = 3
NT = 512
RADIUS = 4
STEP = 0.5
MARK = 8
RANKS = (11, 13, 15, 1, 3, 6, 5, 9, 2, 7, 4, 14, 8, 12, 10, 0)
SHRINKAGE = 0.05
SOURCES = NB * BS
WIDE = NB * 2 * BS
MIB = 1 << 20
VMEM = pl.BlockSpec(memory_space=pltpu.VMEM)
ANY = pl.BlockSpec(memory_space=pl.ANY)


def ranking(devices, local_src):
    fits = devices == len(RANKS) and local_src % 16 == 0 and BS % local_src == 0
    return list(RANKS) if fits else list(range(devices))


def split_table(ranks):
    phases = np.arange(NT)[:, None] * (np.array(ranks) + 1)[None, :] % NT
    angles = phases * (2.0 * math.pi / NT)
    table = np.stack([np.cos(angles), -np.sin(angles)], axis=-1).reshape(NT, 2 * len(ranks)) / math.sqrt(NT)
    table = table.T.astype(np.float32)
    upper = table.astype(jnp.bfloat16)
    lower = (table - upper.astype(np.float32)).astype(jnp.bfloat16)
    return np.concatenate([upper, lower], axis=0)


def row_places(ranks):
    return np.arange(NB, dtype=np.int32) if ranks == sorted(ranks) else np.argsort(ranks).astype(np.int32)


def distances(ranks, local_src):
    sources = (np.array(ranks)[:, None] * local_src + np.arange(local_src)).reshape(-1)
    return np.abs(sources[:, None] - sources[None, :]).astype(np.float32)


def contract(a, b, dims):
    return lax.dot_general(a, b, ((dims[:1], dims[1:]), ((), ())), preferred_element_type=jnp.float32)


def clamp(u):
    return jnp.clip(u, -SHRINKAGE, SHRINKAGE)


def params(limit):
    return pltpu.CompilerParams(vmem_limit_bytes=limit * MIB)


def chunk_rows(rows, most):
    return max(size for size in range(128, most + 1, 128) if rows % size == 0)


def chunks(rows):
    unit = rows // 128 // 6 * 128
    bounds = [0, unit, 2 * unit, 4 * unit, rows] if unit else [0, rows]
    return [slice(low, high) for low, high in zip(bounds[:-1], bounds[1:])]


def build_operator(index_ref, places_ref, multiples_ref, operator_ref):
    operator_ref[...] = jnp.zeros_like(operator_ref)
    runs = places_ref.shape[0] // NB
    length = BS // runs
    for block in range(NB):
        columns = slice(block * 2 * BS, (block + 1) * 2 * BS)
        for band in range(BANDS):
            pair = multiples_ref[block, band]
            turned = jnp.concatenate([-pair[:, BS:], pair[:, :BS]], axis=1)
            for run in range(runs):
                first = pl.multiple_of(places_ref[index_ref[block, band] * runs + run] * length, length)
                part = slice(run * length, (run + 1) * length)
                operator_ref[pl.ds(first, length), columns] = pair[part]
                operator_ref[pl.ds(SOURCES + first, length), columns] = turned[part]


def forward_kernel(
    field_hbm, table_hbm, index_hbm, places_hbm, multiples_hbm, recorded_hbm, radius_hbm, distance_hbm,
    narrow_ref, spectra_ref, field_ref, table_ref, operator_ref, recorded_ref, radius_ref, distance_ref,
    index, places, multiples, loaded, radius, sems, field_sems, *, halves,
):
    count, rows = spectra_ref.shape
    parts = chunks(rows)
    small = [
        pltpu.make_async_copy(table_hbm, table_ref, sems.at[0]),
        pltpu.make_async_copy(index_hbm, index, sems.at[1]),
        pltpu.make_async_copy(multiples_hbm, multiples, sems.at[2]),
        pltpu.make_async_copy(recorded_hbm, loaded, sems.at[3]),
        pltpu.make_async_copy(radius_hbm, radius, sems.at[4]),
        pltpu.make_async_copy(places_hbm, places, sems.at[5]),
        pltpu.make_async_copy(distance_hbm, distance_ref, sems.at[6]),
    ]
    large = []
    for i, part in enumerate(parts):
        place = pl.ds(part.start, part.stop - part.start)
        large.append(pltpu.make_async_copy(field_hbm.at[place], field_ref.at[place], field_sems.at[i]))
    for copy in small[:1] + large[:2] + small[1:] + large[2:]:
        copy.start()

    def transform(i):
        large[i].wait()
        both = contract(table_ref[...], field_ref[parts[i]], (1, 1))
        spectra = both[:count] + both[count:]
        spectra_ref[:, parts[i]] = spectra
        narrow_ref[:, parts[i]] = spectra.astype(jnp.bfloat16)

    small[0].wait()
    transform(0)
    small[1].wait()
    small[2].wait()
    small[5].wait()
    build_operator(index, places, multiples, operator_ref)
    for i in range(1, len(parts) // 2):
        transform(i)
    small[3].wait()
    recorded_ref[...] = loaded[...].astype(jnp.float32)
    for i in range(max(1, len(parts) // 2), len(parts) - 1):
        transform(i)
    small[4].wait()
    shares, amount = max(halves) + 1, radius_ref.shape[1]
    for share in range(shares):
        rows_sent = radius[share * amount : (share + 1) * amount].astype(jnp.float32) + MARK * share
        for rank, half in enumerate(halves):
            if half == share:
                radius_ref[rank] = rows_sent.astype(jnp.bfloat16)
    for i in range(max(1, len(parts) - 1), len(parts)):
        transform(i)
    small[6].wait()


def forward(field, table, block_index, places, multiples, recorded, radius, distance, halves):
    rows, receivers = field.shape[0], radius.shape[1]
    count = table.shape[0] // 2
    arguments = (field, table, block_index, places, multiples, recorded, radius, distance)
    sent = (len(halves), radius.shape[0] // (max(halves) + 1), receivers)
    return pl.pallas_call(
        lambda *refs: forward_kernel(*refs, halves=halves),
        in_specs=[ANY] * 8,
        out_specs=[VMEM] * 8,
        out_shape=[
            jax.ShapeDtypeStruct((count, rows), jnp.bfloat16),
            pltpu.VMEM((count, rows), jnp.float32),
            pltpu.VMEM((rows, NT), jnp.bfloat16),
            pltpu.VMEM(table.shape, jnp.bfloat16),
            pltpu.VMEM((2 * SOURCES, WIDE), jnp.bfloat16),
            pltpu.VMEM((receivers * NB, 2 * BS), jnp.float32),
            jax.ShapeDtypeStruct(sent, jnp.bfloat16),
            pltpu.VMEM(distance.shape, jnp.float32),
        ],
        scratch_shapes=[
            pltpu.SMEM((NB, BANDS), jnp.int32),
            pltpu.SMEM(places.shape, jnp.int32),
            pltpu.VMEM((NB, BANDS, BS, 2 * BS), jnp.bfloat16),
            pltpu.VMEM((receivers * NB, 2 * BS), jnp.bfloat16),
            pltpu.VMEM(radius.shape, jnp.int32),
            pltpu.SemaphoreType.DMA((7,)),
            pltpu.SemaphoreType.DMA((len(chunks(rows)),)),
        ],
        compiler_params=params(16),
        name="forward_dft",
    )(*(pltpu.with_memory_space_constraint(a, pltpu.HBM) for a in arguments))


def gradient_of(returned_ref, table_ref, part):
    returned = returned_ref[:, part]
    return contract(jnp.concatenate([returned, returned], axis=0), table_ref[...], (0, 0))


def middle_kernel(start_ref, returned_ref, spectra_ref, table_ref, field_ref, narrow_ref, *, step):
    count, rows = spectra_ref.shape
    for i in range(rows // step):
        part = slice(i * step, (i + 1) * step)
        update = start_ref[part].astype(jnp.float32) + gradient_of(returned_ref, table_ref, part)
        clamped = clamp(update)
        field_ref[part] = update - clamped
        both = contract(table_ref[...], clamped.astype(jnp.bfloat16), (1, 1))
        linear = spectra_ref[:, part] + 0.5 * returned_ref[:, part].astype(jnp.float32)
        narrow_ref[:, part] = (linear - (both[:count] + both[count:])).astype(jnp.bfloat16)


def middle(start, returned, spectra, table):
    rows = start.shape[0]
    step = chunk_rows(rows, 768)
    return pl.pallas_call(
        lambda *refs: middle_kernel(*refs, step=step),
        in_specs=[VMEM] * 4,
        out_specs=[VMEM] * 2,
        out_shape=[pltpu.VMEM((rows, NT), jnp.float32), jax.ShapeDtypeStruct(spectra.shape, jnp.bfloat16)],
        compiler_params=params(16),
        name="update_and_forward",
    )(start, returned, spectra, table)


def final_kernel(field_ref, returned_ref, table_ref, out_hbm, buffer, sems):
    slots, step, _ = buffer.shape
    rows = field_ref.shape[0]
    copies = []
    for i in range(rows // step):
        if i >= slots:
            copies[i - slots].wait()
        part = slice(i * step, (i + 1) * step)
        update = field_ref[part] + gradient_of(returned_ref, table_ref, part)
        buffer[i % slots] = update - clamp(update)
        copies.append(
            pltpu.make_async_copy(buffer.at[i % slots], out_hbm.at[pl.ds(i * step, step)], sems.at[i % slots])
        )
        copies[i].start()
    for copy in copies[-slots:]:
        copy.wait()


def final(field, returned, table):
    rows = field.shape[0]
    step = chunk_rows(rows, 512)
    slots = min(4, rows // step)
    return pl.pallas_call(
        final_kernel,
        in_specs=[VMEM] * 3,
        out_specs=ANY,
        out_shape=pltpu.HBM((rows, NT), jnp.float32),
        scratch_shapes=[pltpu.VMEM((slots, step, NT), jnp.float32), pltpu.SemaphoreType.DMA((slots,))],
        compiler_params=params(16),
        name="last_update",
    )(field, returned, table)


def smooth(backward, radius, distance, returned_ref):
    sources, receivers = radius.shape
    rows = jnp.concatenate([backward[:sources], backward[sources:]], axis=1)
    narrow = rows.astype(jnp.bfloat16)
    radius = jnp.concatenate([radius, radius], axis=1)
    summed = rows
    for width in range(1, RADIUS + 1):
        band = jnp.where(distance <= width, 1.0, 0.0).astype(jnp.bfloat16)
        summed = jnp.where(radius >= width, contract(band, narrow, (1, 0)), summed)
    smoothed = (summed * (STEP / (2.0 * radius + 1.0))).astype(jnp.bfloat16)
    for part in range(2):
        own = smoothed[:, part * receivers : (part + 1) * receivers]
        if len(returned_ref.shape) == 4:
            returned_ref[:, part] = own.reshape(returned_ref.shape[0], *returned_ref.shape[2:])
        else:
            returned_ref[part * sources : (part + 1) * sources] = own


def adjoint(arrived_ref, operator_ref, recorded_ref):
    operator = operator_ref[...]
    if len(arrived_ref.shape) == 4:
        parts = [arrived_ref[:, part].reshape(SOURCES, arrived_ref.shape[3]) for part in range(2)]
        arrived = jnp.concatenate(parts, axis=0)
    else:
        arrived = arrived_ref[...]
    receivers = recorded_ref.shape[0] // NB
    blocks = [recorded_ref[pl.ds(block, receivers, stride=NB), :] for block in range(NB)]
    residual = jnp.concatenate(blocks, axis=1) - contract(arrived, operator, (0, 0))
    return residual, contract(operator, residual.astype(jnp.bfloat16), (1, 1))


def first_owner_kernel(arrived_ref, operator_ref, recorded_ref, backward_ref):
    _, backward_ref[...] = adjoint(arrived_ref, operator_ref, recorded_ref)


def smooth_kernel(*refs):
    backward_ref, *halves, distance_ref, returned_ref, radius_ref = refs
    if len(halves) == 2:
        own, other = (half[...].astype(jnp.float32) for half in halves)
        both = jnp.stack([jnp.minimum(own, other), jnp.maximum(own, other) - MARK], axis=1)
        radius = both.reshape(radius_ref.shape)
    else:
        radius = halves[0][...].astype(jnp.float32)
    radius_ref[...] = radius
    smooth(backward_ref[...], radius, distance_ref[...], returned_ref)


def last_owner_kernel(
    arrived_ref, operator_ref, recorded_ref, radius_ref, distance_ref, returned_ref, residual_hbm, interleaved, sem
):
    residual, backward = adjoint(arrived_ref, operator_ref, recorded_ref)
    for block in range(NB):
        rows = pl.ds(block, residual.shape[0], stride=NB)
        interleaved[rows, :] = residual[:, block * 2 * BS : (block + 1) * 2 * BS]
    copy = pltpu.make_async_copy(interleaved, residual_hbm, sem)
    copy.start()
    smooth(backward, radius_ref[...], distance_ref[...], returned_ref)
    copy.wait()


def first_owner(arrived, operator, recorded):
    receivers = recorded.shape[0] // NB
    return pl.pallas_call(
        first_owner_kernel,
        in_specs=[VMEM] * 3,
        out_specs=VMEM,
        out_shape=pltpu.VMEM((2 * SOURCES, receivers), jnp.float32),
        compiler_params=params(16),
        cost_estimate=pl.CostEstimate(
            flops=8 * receivers * SOURCES * WIDE, bytes_accessed=8 * receivers * WIDE, transcendentals=0
        ),
        name="owner_products",
    )(arrived, operator, recorded)


def smooth_sources(backward, radius, distance, shape):
    return pl.pallas_call(
        smooth_kernel,
        in_specs=[VMEM] * (2 + len(radius)),
        out_specs=[VMEM] * 2,
        out_shape=[
            jax.ShapeDtypeStruct(shape, jnp.bfloat16),
            pltpu.VMEM((SOURCES, backward.shape[1]), jnp.float32),
        ],
        compiler_params=params(16),
        name="smooth_sources",
    )(backward, *radius, distance)


def last_owner(arrived, operator, recorded, radius, distance, shape):
    receivers = recorded.shape[0] // NB
    return pl.pallas_call(
        last_owner_kernel,
        in_specs=[VMEM] * 5,
        out_specs=[VMEM, ANY],
        out_shape=[
            jax.ShapeDtypeStruct(shape, jnp.bfloat16),
            pltpu.HBM((receivers * NB, 2 * BS), jnp.float32),
        ],
        scratch_shapes=[pltpu.VMEM((receivers * NB, 2 * BS), jnp.float32), pltpu.SemaphoreType.DMA(())],
        compiler_params=params(16),
        name="owner_step",
    )(arrived, operator, recorded, radius, distance)


def on_device(start_field, recorded, multiples, block_index, radius):
    devices = lax.axis_size("freq")
    local_src, receivers, _ = start_field.shape
    rows = local_src * receivers
    ranks = ranking(devices, local_src)
    places = row_places(ranks)
    whole_tiles = local_src % 16 == 0
    sent = (devices, 2, local_src, receivers) if whole_tiles else (2 * SOURCES, receivers)
    shares = 2 if devices % 2 == 0 and local_src % 2 == 0 else 1
    table = jnp.asarray(split_table(ranks))

    def exchange(pieces):
        return lax.all_to_all(pieces, "freq", split_axis=0, concat_axis=0, tiled=True, axis_index_groups=[ranks])

    def by_part(arrived):
        return arrived.reshape(devices, 2, local_src, receivers).swapaxes(0, 1).reshape(2 * SOURCES, receivers)

    def to_owners(narrow):
        arrived = exchange(narrow.reshape(devices, 2, local_src, receivers))
        return arrived if whole_tiles else by_part(arrived)

    def to_owners_with_radius(narrow, radius):
        rows = local_src // shares
        narrow = lax.optimization_barrier(narrow.reshape(devices, 2, local_src, receivers))
        pieces = [
            narrow.reshape(devices, 2 * shares, rows, receivers),
            radius.reshape(devices, 1, rows, receivers),
        ]
        arrived = exchange(jnp.concatenate(pieces, axis=1))
        halves = [arrived[:, 2 * shares]]
        if shares == 2:
            own, other = halves[0], lax.ppermute(halves[0], "freq", [(i, i ^ 1) for i in range(devices)])
            if whole_tiles:
                return by_part(arrived[:, : 2 * shares]), [own, other]
            halves = [jnp.minimum(own, other), jnp.maximum(own, other) - MARK]
        radius = jnp.stack(halves, axis=1).reshape(SOURCES, receivers)
        return by_part(arrived[:, : 2 * shares]), [radius]

    def to_traces(returned):
        if not whole_tiles:
            returned = returned.reshape(2, devices, local_src, receivers).swapaxes(0, 1)
        return exchange(returned).reshape(2 * devices, rows)

    narrow, spectra, start, table, operator, recorded, radius, distance = forward(
        start_field.reshape(rows, NT),
        table,
        block_index,
        jnp.asarray(places),
        multiples[0],
        recorded.reshape(-1, 2 * BS),
        radius,
        jnp.asarray(distances(ranks, local_src)),
        [rank % shares for rank in ranks],
    )
    arrived, radius = to_owners_with_radius(narrow, radius)
    returned, radius = smooth_sources(first_owner(arrived, operator, recorded), radius, distance, sent)
    field, narrow = middle(start, to_traces(returned), spectra, table)
    returned, residual = last_owner(to_owners(narrow), operator, recorded, radius, distance, sent)
    field = final(field, to_traces(returned), table)
    return field.reshape(local_src, receivers, NT), residual.reshape(1, receivers, NB, 2 * BS)


def solution(mesh):
    placed = (
        P(("grp", "freq"), None, None),
        P(("grp", "freq"), None, None, None),
        P(("grp", "freq"), None, None, None, None),
        P(),
        P(("grp", "freq"), None),
    )
    return jax.shard_map(
        on_device,
        mesh=mesh,
        in_specs=placed,
        out_specs=(P(("grp", "freq"), None, None), P(("grp", "freq"), None, None, None)),
        check_vma=False,
    )
```
